32 devices in a mesh: pool: 2 (over x), pencil: 8 (over z, y), tgroup: 2 (over core).
Axes of the slice: x: 2, y: 2, z: 4, core: 2. Of those that a mesh axis runs over, the one named last changes fastest.
Arguments:
- dpsi: float32 [2, 4, 196608], P(None, 'pool', ('pencil', 'tgroup')), parts along dimension 1, may hold values from -6 to 6
- stick_cols: int32 [3072], replicated, may hold values from 0 to 16383, as said below
- pw_z: int32 [3072, 64], P('pencil'), may hold values from 0 to 127, as said below
- v_local: float32 [128, 16384], P('pencil'), may hold values from -6 to 6
- dv: float32 [128, 16384], P('pencil'), may hold values from -6 to 6
Outputs:
- h_dpsi: float32 [2, 4, 196608], P(None, 'pool', ('pencil', 'tgroup')), parts along dimension 1
The draws below stay inside these ranges and needn't reach their ends.
There are 2 independent parts, one for each index of `pool`. The reference program is written for one: setup_inputs(seed, part) draws one part's arguments, and reference() takes and returns one part's arrays. A program takes and returns all parts, laid end to end along the dimension named above; an argument that names none is the same for every part. Nothing has to cross between parts.
Inputs may be any that keep to these rules, and one draw needn't show every extreme that they name: `stick_cols`: the 3072 values are distinct. `pw_z`: the 64 values of each row are distinct.
All inputs are finite; a program needn't handle non-finite values.
Results may differ from the reference program's by a relative error of at most 0.00007.
Values sent between devices are 32-bit elements; how exact they have to be, the bound alone decides.
A program may use at most 128 MiB of HBM per device.

```python
import jax
import jax.numpy as jnp
from jax import lax

N = 128
STICKS = 3072
ZPW = 64
BANDS = 2
NPW = 196608


def draw_stick_cols(key, part):
    column = jnp.arange(N * N, dtype=jnp.int32)
    first = column // N
    second = column % N
    freq_x = jnp.where(first < N // 2, first, first - N)
    freq_y = jnp.where(second < N // 2, second, second - N)
    radius = freq_x * freq_x + freq_y * freq_y
    breaker = jax.random.permutation(jax.random.fold_in(key, 11), N * N).astype(jnp.int32)
    scores = radius * (N * N) + breaker
    chosen = jnp.argsort(scores, stable=True)[:STICKS].astype(jnp.int32)
    return jax.random.permutation(jax.random.fold_in(key, 12), chosen).astype(jnp.int32)


def draw_pw_z(key, part):
    noise = jax.random.randint(jax.random.fold_in(key, 21), (STICKS, N), 0, 2 ** 20)
    scores = noise * N + jnp.arange(N, dtype=jnp.int32)[None, :]
    return jnp.argsort(scores, axis=1, stable=True)[:, :ZPW].astype(jnp.int32)


def steps_of(rng, extent, pieces, least, top_value):
    level = 1.0
    for dim, blocks in pieces:
        steps = jax.random.uniform(jax.random.fold_in(jax.random.fold_in(rng, 6), dim), (blocks,), jnp.float32, least / len(pieces), top_value / len(pieces))
        level = level * jnp.repeat(jnp.exp(steps), extent[dim] // blocks).reshape((-1,) + (1,) * (len(extent) - 1 - dim))
    return level


def bell_draw(own_key, dims, scale, bound, pieces=(), kind=jnp.bfloat16):
    entries = jax.random.normal(own_key, dims, jnp.float32) * scale
    if len(pieces) > 0:
        entries = steps_of(own_key, dims, pieces, -0.22, 0.18) * entries
    return jnp.clip(entries, min=-bound, max=bound).astype(kind)


def setup_inputs(seed: int = 0, part: int = 0) -> dict:
    seeds = jax.random.split(jax.random.key(seed), 6)
    part_keys = jax.random.split(jax.random.fold_in(seeds[5], part), 6)
    return {
        "dpsi": bell_draw(part_keys[0], (2, BANDS, NPW), 1.0, 6.0, ((2, 16),), jnp.float32),
        "stick_cols": draw_stick_cols(jax.random.fold_in(seeds[5], 71), part),
        "pw_z": draw_pw_z(jax.random.fold_in(seeds[5], 71), part),
        "v_local": bell_draw(seeds[3], (N, N * N), 1.0, 6.0, ((0, 8),), jnp.float32),
        "dv": bell_draw(seeds[4], (N, N * N), 0.5, 6.0, ((0, 8),), jnp.float32),
    }


def reference(dpsi, stick_cols, pw_z, v_local, dv):
    potential = (v_local + dv).reshape(N, N, N).transpose(1, 2, 0)
    scale = float(N) ** 1.5
    rows = stick_cols[:, None].astype(jnp.int32)
    depth = pw_z.astype(jnp.int32)

    def one_band(band):
        coeffs = (band[0] + 1j * band[1]).reshape(STICKS, ZPW)
        grid = jnp.zeros((N * N, N), coeffs.dtype).at[rows, depth].set(coeffs)
        wave = jnp.fft.ifftn(grid.reshape(N, N, N)) * scale
        result = jnp.fft.fftn(potential * wave) / scale
        picked = result.reshape(N * N, N)[rows, depth].reshape(NPW)
        return jnp.stack([jnp.real(picked), jnp.imag(picked)])

    output = lax.map(one_band, dpsi.transpose(1, 0, 2))
    return output.transpose(1, 0, 2)
```

```python
from functools import partial
import math

import jax
import jax.numpy as jnp
import ml_dtypes
import numpy as np
from jax import lax
from jax.experimental import pallas as pl
from jax.experimental.pallas import tpu as pltpu
from jax.sharding import PartitionSpec as P

F32 = jnp.float32
BF16 = jnp.bfloat16
LANES = 128
GROUP = 8


def halves(table):
    hi = table.astype(ml_dtypes.bfloat16)
    lo = (table - hi.astype(np.float64)).astype(ml_dtypes.bfloat16)
    return jnp.asarray(hi), jnp.asarray(lo)


def split(value):
    hi = value.astype(BF16)
    lo = (value - hi.astype(F32)).astype(BF16)
    return hi, lo


def dot3(left, right, dims=((1,), (0,))):
    mul = lambda a, b: lax.dot_general(a, b, (dims, ((), ())), preferred_element_type=F32)
    return mul(left[0], right[0]) + (mul(left[0], right[1]) + mul(left[1], right[0]))


def waves(length):
    k = np.arange(length)
    angle = (k[:, None] * k[None, :] % length) * (2.0 * math.pi / length)
    return np.cos(angle) / math.sqrt(length), np.sin(angle) / math.sqrt(length)


def depth_table(length, devices):
    cos, sin = waves(length)
    planes = length // devices
    whole = np.stack([np.stack([cos, -sin], 1), np.stack([sin, cos], 1)])
    whole = whole.reshape(2, devices, planes, 2 * length)
    return whole.transpose(1, 0, 2, 3).reshape(2 * length, 2 * length)


def row_tables(length):
    cos, sin = waves(length)
    return np.concatenate([cos, sin]), np.concatenate([cos, -sin])


def column_table(length, slots):
    cos, sin = waves(length)
    whole = np.stack([np.stack([cos, -sin], 1), np.stack([sin, cos], 1)])
    whole = whole.reshape(2, length, 2, slots, length // slots)
    return whole.transpose(0, 1, 4, 2, 3).reshape(2 * length, 2 * length)


def depth_up(coeff_ref, pw_ref, table_hi, table_lo, out_ref):
    _, bands, rows, width = coeff_ref.shape
    devices, part_rows, _ = out_ref.shape
    zpw = width // 2
    pw = pw_ref[...]
    z = lax.broadcasted_iota(jnp.int32, (rows, LANES), 1)
    pieces = [[None] * 2 for _ in range(bands)]
    for parity in range(2):
        source = jnp.full((rows, LANES), -1, jnp.int32)
        for k in range(parity * zpw, (parity + 1) * zpw):
            source = jnp.where(pw[:, k : k + 1] == z, k, source)
        found = source >= 0
        source = jnp.maximum(source, 0)
        for band in range(bands):
            parts = []
            for part in range(2):
                taken = jnp.take_along_axis(
                    coeff_ref[part, band], source, axis=1, mode="promise_in_bounds"
                )
                parts.append(jnp.where(found, taken, 0.0))
            pieces[band][parity] = jnp.concatenate(parts, axis=1)
    column = jnp.concatenate([piece for pair in pieces for piece in pair], axis=0)
    field = dot3((table_hi[...], table_lo[...]), split(column), ((1,), (1,)))
    for device in range(devices):
        out_ref[device] = field[device * part_rows : (device + 1) * part_rows]


def depth_down(field_ref, pw_ref, table_hi, table_lo, out_ref, flat):
    _, bands, rows, width = out_ref.shape
    devices, part_rows, _ = field_ref.shape
    length = devices * part_rows // 2
    for device in range(devices):
        flat[device * part_rows : (device + 1) * part_rows] = field_ref[device]
    column = dot3(
        split(flat[...]), (table_hi[...], table_lo[...]), ((0,), (0,))
    )
    pw = pw_ref[...]
    first = lax.broadcasted_iota(jnp.int32, (rows, LANES), 1) < width // 2
    for band in range(bands):
        for part in range(2):
            taken = []
            for parity in range(2):
                start = (band * 2 + parity) * rows
                piece = column[start : start + rows, part * length : (part + 1) * length]
                taken.append(
                    jnp.take_along_axis(piece, pw, axis=1, mode="promise_in_bounds")
                )
            out_ref[part, band] = jnp.where(first, taken[0], taken[1])


def turn(value):
    half = value.shape[0] // 2
    return jnp.concatenate([-value[half:], value[:half]], axis=0)


def plane_kernel(
    bands,
    cols_ref,
    field_ref,
    weight_ref,
    up_hi,
    up_lo,
    down_hi,
    down_lo,
    column_hi,
    column_lo,
    back_hi,
    back_lo,
    out_ref,
    flat,
    sticks,
    grid,
):
    devices, part_rows, block = field_ref.shape
    planes = part_rows // 2
    own = block // bands
    pairs = own // 2
    length = weight_ref.shape[1]
    bz = bands * planes
    slots = LANES // (2 * bz)
    inner = length // slots
    group_rows = inner * length
    total = devices * own

    grid[...] = jnp.zeros_like(grid)
    for device in range(devices):
        for part in range(2):
            for band in range(bands):
                flat[
                    (part * bands + band) * planes : (part * bands + band + 1) * planes,
                    device * own : (device + 1) * own,
                ] = field_ref[
                    device, part * planes : (part + 1) * planes, band * own : (band + 1) * own
                ]
    for tile in range(total // LANES):
        value = flat[:, tile * LANES : (tile + 1) * LANES]
        value = jnp.concatenate([value[:bz]] * slots + [value[bz:]] * slots, axis=0)
        sticks[tile * LANES : (tile + 1) * LANES] = value.T

    lane = lax.broadcasted_iota(jnp.int32, (1, LANES), 1)
    slot_of_lane = lane // bz % slots
    chunks = pairs // GROUP

    def each_stick(act):
        @pl.loop(0, devices * chunks)
        def _(step):
            device = step // chunks
            start = (step - device * chunks) * GROUP
            for parity in range(2):
                base = pl.multiple_of(device * own + parity * pairs + start, GROUP)
                for i in range(GROUP):
                    col = cols_ref[device * own + 2 * (start + i) + parity]
                    act(base + i, col & (group_rows - 1), slot_of_lane == col // group_rows)

    def put(stick, row, mask):
        pltpu.store(grid.at[pl.ds(row, 1), :], sticks[pl.ds(stick, 1), :], mask=mask)

    each_stick(put)

    @pl.loop(0, inner)
    def _(x):
        rows = pl.ds(pl.multiple_of(x * length, length), length)
        hi, lo = split(grid[rows, :].T)
        hi = jnp.concatenate([hi, turn(hi)], axis=1)
        lo = jnp.concatenate([lo, turn(lo)], axis=1)
        grid[rows, :] = dot3((hi, lo), (up_hi[...], up_lo[...]))

    for z in range(planes):
        picks = [pl.ds(band * planes + z, 2 * length, stride=bz) for band in range(bands)]
        value = jnp.concatenate([grid[pick, :] for pick in picks], axis=1)
        value = dot3((column_hi[...], column_lo[...]), split(value))
        weight = weight_ref[z]
        weight = jnp.concatenate([weight] * 2, axis=0)
        weight = jnp.concatenate([weight] * bands, axis=1)
        value = dot3((back_hi[...], back_lo[...]), split(value * weight))
        for band, pick in enumerate(picks):
            grid[pick, :] = value[:, band * length : (band + 1) * length]

    @pl.loop(0, inner)
    def _(x):
        rows = pl.ds(pl.multiple_of(x * length, length), length)
        hi, lo = split(grid[rows, :])
        hi = jnp.concatenate([hi, turn(hi)], axis=1)
        lo = jnp.concatenate([lo, turn(lo)], axis=1)
        grid[rows, :] = dot3((hi, lo), (down_hi[...], down_lo[...])).T

    def get(stick, row, mask):
        sticks[pl.ds(stick, 1), :] = jnp.where(mask, grid[pl.ds(row, 1), :], 0.0)

    each_stick(get)

    for tile in range(total // LANES):
        value = sticks[tile * LANES : (tile + 1) * LANES].T
        half = slots * bz
        sums = []
        for part in range(2):
            terms = [
                value[part * half + slot * bz : part * half + (slot + 1) * bz]
                for slot in range(slots)
            ]
            sums.append(sum(terms[1:], terms[0]))
        flat[:, tile * LANES : (tile + 1) * LANES] = jnp.concatenate(sums, axis=0)
    for device in range(devices):
        for part in range(2):
            for band in range(bands):
                out_ref[
                    device, part * planes : (part + 1) * planes, band * own : (band + 1) * own
                ] = flat[
                    (part * bands + band) * planes : (part * bands + band + 1) * planes,
                    device * own : (device + 1) * own,
                ]


VM = pl.BlockSpec(memory_space=pltpu.VMEM)
SM = pl.BlockSpec(memory_space=pltpu.SMEM)
PARAMS = pltpu.CompilerParams(vmem_limit_bytes=48 * 1024 * 1024)


def local(dpsi, stick_cols, pw_z, v_local, dv):
    devices = lax.axis_size("pencil") * lax.axis_size("tgroup")
    cores = lax.axis_size("tgroup")
    core = lax.axis_index("tgroup")
    length = math.isqrt(v_local.shape[1])
    planes = v_local.shape[0] // cores
    own = pw_z.shape[0] // cores
    zpw = pw_z.shape[1]
    bands = dpsi.shape[1]
    pairs = own // 2
    bz = bands * planes
    slots = LANES // (2 * bz)

    potential = lax.dynamic_slice_in_dim(v_local, core * planes, planes, 0)
    potential = potential + lax.dynamic_slice_in_dim(dv, core * planes, planes, 0)
    potential = potential.reshape(planes, length, length)
    rows = lax.dynamic_slice_in_dim(pw_z, core * own, own, 0).reshape(pairs, 2 * zpw)
    coeff = dpsi.reshape(2, bands, pairs, 2 * zpw)

    depth = halves(depth_table(length, devices))
    up, down = [halves(table) for table in row_tables(length)]
    column = column_table(length, slots)
    back = halves(np.ascontiguousarray(column.T))
    column = halves(column)

    travel = jax.ShapeDtypeStruct((devices, 2 * planes, bands * own), F32)
    field = pl.pallas_call(
        depth_up, out_shape=travel, in_specs=[VM] * 4, out_specs=VM, compiler_params=PARAMS
    )(coeff, rows, *depth)
    swap = partial(
        lax.all_to_all,
        axis_name=("pencil", "tgroup"),
        split_axis=0,
        concat_axis=0,
        tiled=True,
    )
    field = swap(field)
    field = pl.pallas_call(
        partial(plane_kernel, bands),
        out_shape=travel,
        in_specs=[SM] + [VM] * 10,
        out_specs=VM,
        scratch_shapes=[
            pltpu.VMEM((2 * bz, devices * own), F32),
            pltpu.VMEM((devices * own, LANES), F32),
            pltpu.VMEM((length // slots * length, LANES), F32),
        ],
        compiler_params=PARAMS,
    )(stick_cols, field, potential, *up, *down, *column, *back)
    field = swap(field)
    output = pl.pallas_call(
        depth_down,
        out_shape=jax.ShapeDtypeStruct(coeff.shape, F32),
        in_specs=[VM] * 4,
        out_specs=VM,
        scratch_shapes=[pltpu.VMEM((2 * length, bands * own), F32)],
        compiler_params=PARAMS,
    )(field, rows, *depth)
    return output.reshape(dpsi.shape)


def solution(mesh):
    in_specs = (
        P(None, "pool", ("pencil", "tgroup")),
        P(),
        P("pencil", None),
        P("pencil", None),
        P("pencil", None),
    )
    out_specs = P(None, "pool", ("pencil", "tgroup"))
    return jax.shard_map(local, mesh=mesh, in_specs=in_specs, out_specs=out_specs, check_vma=False)
```

```python
from functools import partial
import math

import jax
import jax.numpy as jnp
import ml_dtypes
import numpy as np
from jax import lax
from jax.experimental import pallas as pl
from jax.experimental.pallas import tpu as pltpu
from jax.sharding import PartitionSpec as P

F32 = jnp.float32
BF16 = jnp.bfloat16
LANES = 128
GROUP = 8


def halves(table):
    hi = table.astype(ml_dtypes.bfloat16)
    lo = (table - hi.astype(np.float64)).astype(ml_dtypes.bfloat16)
    return jnp.asarray(hi), jnp.asarray(lo)


def split(value):
    hi = value.astype(BF16)
    lo = (value - hi.astype(F32)).astype(BF16)
    return hi, lo


def dot3(left, right, dims=((1,), (0,))):
    mul = lambda a, b: lax.dot_general(a, b, (dims, ((), ())), preferred_element_type=F32)
    return mul(left[0], right[0]) + (mul(left[0], right[1]) + mul(left[1], right[0]))


def waves(length):
    k = np.arange(length)
    angle = (k[:, None] * k[None, :] % length) * (2.0 * math.pi / length)
    return np.cos(angle) / math.sqrt(length), np.sin(angle) / math.sqrt(length)


def depth_table(length, devices):
    cos, sin = waves(length)
    planes = length // devices
    whole = np.stack([np.stack([cos, -sin], 1), np.stack([sin, cos], 1)])
    whole = whole.reshape(2, devices, planes, 2 * length)
    return whole.transpose(1, 0, 2, 3).reshape(2 * length, 2 * length)


def row_tables(length):
    cos, sin = waves(length)
    return np.concatenate([cos, sin]), np.concatenate([cos, -sin])


def column_table(length, slots):
    cos, sin = waves(length)
    whole = np.stack([np.stack([cos, -sin], 1), np.stack([sin, cos], 1)])
    whole = whole.reshape(2, length, 2, slots, length // slots)
    return whole.transpose(0, 1, 4, 2, 3).reshape(2 * length, 2 * length)


def depth_up(coeff_ref, pw_ref, table_hi, table_lo, out_ref):
    _, bands, rows, width = coeff_ref.shape
    devices, part_rows, _ = out_ref.shape
    zpw = width // 2
    pw = pw_ref[...]
    z = lax.broadcasted_iota(jnp.int32, (rows, LANES), 1)
    pieces = [[None] * 2 for _ in range(bands)]
    for parity in range(2):
        source = jnp.full((rows, LANES), -1, jnp.int32)
        for k in range(parity * zpw, (parity + 1) * zpw):
            source = jnp.where(pw[:, k : k + 1] == z, k, source)
        found = source >= 0
        source = jnp.maximum(source, 0)
        for band in range(bands):
            parts = []
            for part in range(2):
                taken = jnp.take_along_axis(
                    coeff_ref[part, band], source, axis=1, mode="promise_in_bounds"
                )
                parts.append(jnp.where(found, taken, 0.0))
            pieces[band][parity] = jnp.concatenate(parts, axis=1)
    column = jnp.concatenate([piece for pair in pieces for piece in pair], axis=0)
    field = dot3((table_hi[...], table_lo[...]), split(column), ((1,), (1,)))
    for device in range(devices):
        out_ref[device] = field[device * part_rows : (device + 1) * part_rows]


def depth_down(field_ref, pw_ref, table_hi, table_lo, out_ref, flat):
    _, bands, rows, width = out_ref.shape
    devices, part_rows, _ = field_ref.shape
    length = devices * part_rows // 2
    for device in range(devices):
        flat[device * part_rows : (device + 1) * part_rows] = field_ref[device]
    column = dot3(
        split(flat[...]), (table_hi[...], table_lo[...]), ((0,), (0,))
    )
    pw = pw_ref[...]
    first = lax.broadcasted_iota(jnp.int32, (rows, LANES), 1) < width // 2
    for band in range(bands):
        for part in range(2):
            taken = []
            for parity in range(2):
                start = (band * 2 + parity) * rows
                piece = column[start : start + rows, part * length : (part + 1) * length]
                taken.append(
                    jnp.take_along_axis(piece, pw, axis=1, mode="promise_in_bounds")
                )
            out_ref[part, band] = jnp.where(first, taken[0], taken[1])


def turn(value):
    half = value.shape[0] // 2
    return jnp.concatenate([-value[half:], value[:half]], axis=0)


def plane_kernel(
    bands,
    cols_ref,
    field_ref,
    weight_ref,
    up_hi,
    up_lo,
    down_hi,
    down_lo,
    column_hi,
    column_lo,
    back_hi,
    back_lo,
    out_ref,
    flat,
    sticks,
    grid,
):
    devices, part_rows, block = field_ref.shape
    planes = part_rows // 2
    own = block // bands
    pairs = own // 2
    length = weight_ref.shape[1]
    bz = bands * planes
    slots = LANES // (2 * bz)
    inner = length // slots
    group_rows = inner * length
    batch = math.gcd(inner, 4)
    total = devices * own

    grid[...] = jnp.zeros_like(grid)
    for device in range(devices):
        for part in range(2):
            for band in range(bands):
                flat[
                    (part * bands + band) * planes : (part * bands + band + 1) * planes,
                    device * own : (device + 1) * own,
                ] = field_ref[
                    device, part * planes : (part + 1) * planes, band * own : (band + 1) * own
                ]
    for tile in range(total // LANES):
        value = flat[:, tile * LANES : (tile + 1) * LANES]
        value = jnp.concatenate([value[:bz]] * slots + [value[bz:]] * slots, axis=0)
        sticks[tile * LANES : (tile + 1) * LANES] = value.T

    lane = lax.broadcasted_iota(jnp.int32, (1, LANES), 1)
    slot_of_lane = lane // bz % slots
    chunks = pairs // GROUP

    shift = group_rows.bit_length() - 1

    def each_group(act):
        @pl.loop(0, devices * chunks)
        def _(step):
            device = lax.div(step, chunks)
            start = (step - device * chunks) * GROUP
            first = device * own + 2 * start
            cols = [cols_ref[first + i] for i in range(2 * GROUP)]
            rows = [col & (group_rows - 1) for col in cols]
            masks = [slot_of_lane == lax.shift_right_logical(col, shift) for col in cols]
            base = pl.multiple_of(device * own + start, GROUP)
            places = []
            for i in range(2 * GROUP):
                places.append(base + (i % 2) * pairs + i // 2)
            act(places, rows, masks)

    def put(places, rows, masks):
        values = [sticks[pl.ds(place, 1), :] for place in places]
        for value, row, mask in zip(values, rows, masks):
            pltpu.store(grid.at[pl.ds(row, 1), :], value, mask=mask)

    each_group(put)

    @pl.loop(0, inner // batch)
    def _(step):
        whole = pl.ds(pl.multiple_of(step * batch * length, batch * length), batch * length)
        his, los = [], []
        for i in range(batch):
            start = pl.multiple_of((step * batch + i) * length, length)
            hi, lo = split(grid[pl.ds(start, length), :].T)
            his.append(jnp.concatenate([hi, turn(hi)], axis=1))
            los.append(jnp.concatenate([lo, turn(lo)], axis=1))
        pair = (jnp.concatenate(his, axis=0), jnp.concatenate(los, axis=0))
        grid[whole, :] = dot3(pair, (up_hi[...], up_lo[...]))

    for z in range(planes):
        picks = [pl.ds(band * planes + z, 2 * length, stride=bz) for band in range(bands)]
        value = jnp.concatenate([grid[pick, :] for pick in picks], axis=1)
        value = dot3((column_hi[...], column_lo[...]), split(value))
        weight = weight_ref[z]
        weight = jnp.concatenate([weight] * 2, axis=0)
        weight = jnp.concatenate([weight] * bands, axis=1)
        value = dot3((back_hi[...], back_lo[...]), split(value * weight))
        for band, pick in enumerate(picks):
            grid[pick, :] = value[:, band * length : (band + 1) * length]

    @pl.loop(0, inner // batch)
    def _(step):
        his, los = [], []
        starts = [pl.multiple_of((step * batch + i) * length, length) for i in range(batch)]
        for start in starts:
            hi, lo = split(grid[pl.ds(start, length), :])
            his.append(jnp.concatenate([hi, turn(hi)], axis=1))
            los.append(jnp.concatenate([lo, turn(lo)], axis=1))
        pair = (jnp.concatenate(his, axis=0), jnp.concatenate(los, axis=0))
        value = dot3(pair, (down_hi[...], down_lo[...]))
        for i, start in enumerate(starts):
            grid[pl.ds(start, length), :] = value[i * length : (i + 1) * length].T

    def get(places, rows, masks):
        values = [grid[pl.ds(row, 1), :] for row in rows]
        for value, place, mask in zip(values, places, masks):
            sticks[pl.ds(place, 1), :] = jnp.where(mask, value, 0.0)

    each_group(get)

    for tile in range(total // LANES):
        value = sticks[tile * LANES : (tile + 1) * LANES].T
        half = slots * bz
        sums = []
        for part in range(2):
            terms = [
                value[part * half + slot * bz : part * half + (slot + 1) * bz]
                for slot in range(slots)
            ]
            sums.append(sum(terms[1:], terms[0]))
        flat[:, tile * LANES : (tile + 1) * LANES] = jnp.concatenate(sums, axis=0)
    for device in range(devices):
        for part in range(2):
            for band in range(bands):
                out_ref[
                    device, part * planes : (part + 1) * planes, band * own : (band + 1) * own
                ] = flat[
                    (part * bands + band) * planes : (part * bands + band + 1) * planes,
                    device * own : (device + 1) * own,
                ]


VM = pl.BlockSpec(memory_space=pltpu.VMEM)
SM = pl.BlockSpec(memory_space=pltpu.SMEM)
PARAMS = pltpu.CompilerParams(vmem_limit_bytes=48 * 1024 * 1024)


def local(dpsi, stick_cols, pw_z, v_local, dv):
    devices = lax.axis_size("pencil") * lax.axis_size("tgroup")
    cores = lax.axis_size("tgroup")
    core = lax.axis_index("tgroup")
    length = math.isqrt(v_local.shape[1])
    planes = v_local.shape[0] // cores
    own = pw_z.shape[0] // cores
    zpw = pw_z.shape[1]
    bands = dpsi.shape[1]
    pairs = own // 2
    bz = bands * planes
    slots = LANES // (2 * bz)

    potential = lax.dynamic_slice_in_dim(v_local, core * planes, planes, 0)
    potential = potential + lax.dynamic_slice_in_dim(dv, core * planes, planes, 0)
    potential = potential.reshape(planes, length, length)
    rows = lax.dynamic_slice_in_dim(pw_z, core * own, own, 0).reshape(pairs, 2 * zpw)
    coeff = dpsi.reshape(2, bands, pairs, 2 * zpw)

    depth = halves(depth_table(length, devices))
    up, down = [halves(table) for table in row_tables(length)]
    column = column_table(length, slots)
    back = halves(np.ascontiguousarray(column.T))
    column = halves(column)

    travel = jax.ShapeDtypeStruct((devices, 2 * planes, bands * own), F32)
    field = pl.pallas_call(
        depth_up, out_shape=travel, in_specs=[VM] * 4, out_specs=VM, compiler_params=PARAMS
    )(coeff, rows, *depth)
    swap = partial(
        lax.all_to_all,
        axis_name=("pencil", "tgroup"),
        split_axis=0,
        concat_axis=0,
        tiled=True,
    )
    field = swap(field)
    field = pl.pallas_call(
        partial(plane_kernel, bands),
        out_shape=travel,
        in_specs=[SM] + [VM] * 10,
        out_specs=VM,
        scratch_shapes=[
            pltpu.VMEM((2 * bz, devices * own), F32),
            pltpu.VMEM((devices * own, LANES), F32),
            pltpu.VMEM((length // slots * length, LANES), F32),
        ],
        compiler_params=PARAMS,
    )(stick_cols, field, potential, *up, *down, *column, *back)
    field = swap(field)
    output = pl.pallas_call(
        depth_down,
        out_shape=jax.ShapeDtypeStruct(coeff.shape, F32),
        in_specs=[VM] * 4,
        out_specs=VM,
        scratch_shapes=[pltpu.VMEM((2 * length, bands * own), F32)],
        compiler_params=PARAMS,
    )(field, rows, *depth)
    return output.reshape(dpsi.shape)


def solution(mesh):
    in_specs = (
        P(None, "pool", ("pencil", "tgroup")),
        P(),
        P("pencil", None),
        P("pencil", None),
        P("pencil", None),
    )
    out_specs = P(None, "pool", ("pencil", "tgroup"))
    return jax.shard_map(local, mesh=mesh, in_specs=in_specs, out_specs=out_specs, check_vma=False)
```

```python
from functools import partial
import math

import jax
import jax.numpy as jnp
import ml_dtypes
import numpy as np
from jax import lax
from jax.experimental import pallas as pl
from jax.experimental.pallas import tpu as pltpu
from jax.sharding import PartitionSpec as P

F32 = jnp.float32
BF16 = jnp.bfloat16
LANES = 128
GROUP = 8


def halves(table):
    hi = table.astype(ml_dtypes.bfloat16)
    lo = (table - hi.astype(np.float64)).astype(ml_dtypes.bfloat16)
    return jnp.asarray(hi), jnp.asarray(lo)


def split(value):
    hi = value.astype(BF16)
    lo = (value - hi.astype(F32)).astype(BF16)
    return hi, lo


def dot3(left, right, dims=((1,), (0,))):
    mul = lambda a, b: lax.dot_general(a, b, (dims, ((), ())), preferred_element_type=F32)
    return mul(left[0], right[0]) + (mul(left[0], right[1]) + mul(left[1], right[0]))


def waves(length):
    k = np.arange(length)
    angle = (k[:, None] * k[None, :] % length) * (2.0 * math.pi / length)
    return np.cos(angle) / math.sqrt(length), np.sin(angle) / math.sqrt(length)


def depth_table(length, devices):
    cos, sin = waves(length)
    planes = length // devices
    whole = np.stack([np.stack([cos, -sin], 1), np.stack([sin, cos], 1)])
    whole = whole.reshape(2, devices, planes, 2 * length)
    return whole.transpose(1, 0, 2, 3).reshape(2 * length, 2 * length)


def row_tables(length):
    cos, sin = waves(length)
    return np.concatenate([cos, sin]), np.concatenate([cos, -sin])


def column_table(length, slots):
    cos, sin = waves(length)
    whole = np.stack([np.stack([cos, -sin], 1), np.stack([sin, cos], 1)])
    whole = whole.reshape(2, length, 2, slots, length // slots)
    return whole.transpose(0, 1, 4, 2, 3).reshape(2 * length, 2 * length)


class Peers:
    def __init__(self):
        self.cores = lax.axis_size("tgroup")
        self.count = lax.axis_size("pencil") * self.cores
        self.me = lax.axis_index("pencil") * self.cores + lax.axis_index("tgroup")
        self.barrier = pltpu.get_barrier_semaphore()

    def at(self, step):
        return lax.rem(self.me + step, self.count)

    def name(self, device):
        return {"pencil": lax.div(device, self.cores), "tgroup": lax.rem(device, self.cores)}

    def greet(self):
        @pl.loop(1, self.count)
        def _(step):
            pl.semaphore_signal(
                self.barrier,
                inc=1,
                device_id=self.name(self.at(step)),
                device_id_type=pl.DeviceIdType.MESH,
            )

    def met(self):
        pl.semaphore_wait(self.barrier, self.count - 1)

    def copy(self, step, source, target, sent, got):
        peer = self.at(step)
        return pltpu.make_async_remote_copy(
            src_ref=source.at[peer],
            dst_ref=target.at[self.me],
            send_sem=sent.at[step],
            recv_sem=got.at[step],
            device_id=self.name(peer),
            device_id_type=pl.DeviceIdType.MESH,
        )

    def settle(self, source, target, sent, got):
        @pl.loop(1, self.count)
        def _(step):
            self.copy(step, source, target, sent, got).wait()


def depth_up(
    coeff_ref,
    pw_ref,
    table_hi,
    table_lo,
    local_ref,
    change_ref,
    out_ref,
    weight_ref,
    ready,
    first,
    second,
    sent,
    got,
    loads,
):
    peers = Peers()
    peers.greet()
    fetch = [
        pltpu.make_async_copy(local_ref, first, loads.at[0]),
        pltpu.make_async_copy(change_ref, second, loads.at[1]),
    ]
    for copy in fetch:
        copy.start()
    _, bands, rows, width = coeff_ref.shape
    devices, part_rows, _ = out_ref.shape
    zpw = width // 2
    pw = pw_ref[...]
    z = lax.broadcasted_iota(jnp.int32, (rows, LANES), 1)
    pieces = [[None] * 2 for _ in range(bands)]
    for parity in range(2):
        source = jnp.full((rows, LANES), -1, jnp.int32)
        for k in range(parity * zpw, (parity + 1) * zpw):
            source = jnp.where(pw[:, k : k + 1] == z, k, source)
        found = source >= 0
        source = jnp.maximum(source, 0)
        for band in range(bands):
            parts = []
            for part in range(2):
                taken = jnp.take_along_axis(
                    coeff_ref[part, band], source, axis=1, mode="promise_in_bounds"
                )
                parts.append(jnp.where(found, taken, 0.0))
            pieces[band][parity] = jnp.concatenate(parts, axis=1)
    column = jnp.concatenate([piece for pair in pieces for piece in pair], axis=0)
    field = dot3((table_hi[...], table_lo[...]), split(column), ((1,), (1,)))
    for device in range(devices):
        ready[device] = field[device * part_rows : (device + 1) * part_rows]
    peers.met()

    @pl.loop(1, devices)
    def _(step):
        peers.copy(step, ready, out_ref, sent, got).start()

    out_ref[peers.me] = ready[peers.me]
    for copy in fetch:
        copy.wait()
    planes = part_rows // 2
    core = lax.axis_index("tgroup")
    for x in range(weight_ref.shape[0] // planes):
        lanes = slice(x * LANES, (x + 1) * LANES)
        whole = first[:, lanes] + second[:, lanes]
        mine = whole[:planes]
        for other in range(1, peers.cores):
            mine = jnp.where(core == other, whole[other * planes : (other + 1) * planes], mine)
        weight_ref[x * planes : (x + 1) * planes] = mine
    peers.settle(ready, out_ref, sent, got)


def turn(value):
    half = value.shape[0] // 2
    return jnp.concatenate([-value[half:], value[:half]], axis=0)


def plane_kernel(
    bands,
    cols_ref,
    field_ref,
    weight_ref,
    up_hi,
    up_lo,
    down_hi,
    down_lo,
    column_hi,
    column_lo,
    back_hi,
    back_lo,
    grid,
    flat,
    sticks,
):
    devices, part_rows, block = field_ref.shape
    planes = part_rows // 2
    own = block // bands
    pairs = own // 2
    length = weight_ref.shape[1]
    bz = bands * planes
    slots = LANES // (2 * bz)
    inner = length // slots
    group_rows = inner * length
    batch = math.gcd(inner, 4)
    total = devices * own
    shift = group_rows.bit_length() - 1

    grid[...] = jnp.zeros_like(grid)
    for device in range(devices):
        for part in range(2):
            for band in range(bands):
                flat[
                    (part * bands + band) * planes : (part * bands + band + 1) * planes,
                    device * own : (device + 1) * own,
                ] = field_ref[
                    device, part * planes : (part + 1) * planes, band * own : (band + 1) * own
                ]
    for tile in range(total // LANES):
        value = flat[:, tile * LANES : (tile + 1) * LANES]
        value = jnp.concatenate([value[:bz]] * slots + [value[bz:]] * slots, axis=0)
        sticks[tile * LANES : (tile + 1) * LANES] = value.T

    lane = lax.broadcasted_iota(jnp.int32, (1, LANES), 1)
    slot_of_lane = lane // bz % slots
    chunks = pairs // GROUP

    @pl.loop(0, devices * chunks)
    def _(step):
        device = lax.div(step, chunks)
        start = (step - device * chunks) * GROUP
        first = device * own + 2 * start
        cols = [cols_ref[first + i] for i in range(2 * GROUP)]
        rows = [col & (group_rows - 1) for col in cols]
        masks = [slot_of_lane == lax.shift_right_logical(col, shift) for col in cols]
        base = pl.multiple_of(device * own + start, GROUP)
        places = [base + (i % 2) * pairs + i // 2 for i in range(2 * GROUP)]
        values = [sticks[pl.ds(place, 1), :] for place in places]
        for value, row, mask in zip(values, rows, masks):
            pltpu.store(grid.at[pl.ds(row, 1), :], value, mask=mask)

    @pl.loop(0, inner // batch)
    def _(step):
        whole = pl.ds(pl.multiple_of(step * batch * length, batch * length), batch * length)
        his, los = [], []
        for i in range(batch):
            start = pl.multiple_of((step * batch + i) * length, length)
            hi, lo = split(grid[pl.ds(start, length), :].T)
            his.append(jnp.concatenate([hi, turn(hi)], axis=1))
            los.append(jnp.concatenate([lo, turn(lo)], axis=1))
        pair = (jnp.concatenate(his, axis=0), jnp.concatenate(los, axis=0))
        grid[whole, :] = dot3(pair, (up_hi[...], up_lo[...]))

    for z in range(planes):
        picks = [pl.ds(band * planes + z, 2 * length, stride=bz) for band in range(bands)]
        value = jnp.concatenate([grid[pick, :] for pick in picks], axis=1)
        value = dot3((column_hi[...], column_lo[...]), split(value))
        weight = weight_ref[pl.ds(z, length, stride=planes), :]
        weight = jnp.concatenate([weight] * 2, axis=0)
        weight = jnp.concatenate([weight] * bands, axis=1)
        value = dot3((back_hi[...], back_lo[...]), split(value * weight))
        for band, pick in enumerate(picks):
            grid[pick, :] = value[:, band * length : (band + 1) * length]

    @pl.loop(0, inner // batch)
    def _(step):
        his, los = [], []
        starts = [pl.multiple_of((step * batch + i) * length, length) for i in range(batch)]
        for start in starts:
            hi, lo = split(grid[pl.ds(start, length), :])
            his.append(jnp.concatenate([hi, turn(hi)], axis=1))
            los.append(jnp.concatenate([lo, turn(lo)], axis=1))
        pair = (jnp.concatenate(his, axis=0), jnp.concatenate(los, axis=0))
        value = dot3(pair, (down_hi[...], down_lo[...]))
        for i, start in enumerate(starts):
            grid[pl.ds(start, length), :] = value[i * length : (i + 1) * length].T


def depth_down(
    cols_ref,
    grid_ref,
    pw_ref,
    table_hi,
    table_lo,
    out_ref,
    ready,
    field,
    sticks,
    flat,
    sent,
    got,
):
    peers = Peers()
    peers.greet()
    _, bands, rows, width = out_ref.shape
    devices, part_rows, _ = ready.shape
    planes = part_rows // 2
    own = 2 * rows
    length = devices * planes
    bz = bands * planes
    slots = LANES // (2 * bz)
    half = slots * bz
    group_rows = grid_ref.shape[0]
    shift = group_rows.bit_length() - 1
    lane = lax.broadcasted_iota(jnp.int32, (1, LANES), 1)
    slot_of_lane = lane // bz % slots

    def gather(device):
        @pl.loop(0, rows // GROUP)
        def _(chunk):
            start = pl.multiple_of(chunk * GROUP, GROUP)
            first = device * own + 2 * start
            cols = [cols_ref[first + i] for i in range(2 * GROUP)]
            masks = [slot_of_lane == lax.shift_right_logical(col, shift) for col in cols]
            values = [grid_ref[pl.ds(col & (group_rows - 1), 1), :] for col in cols]
            for i, (value, mask) in enumerate(zip(values, masks)):
                sticks[pl.ds(start + (i % 2) * rows + i // 2, 1), :] = jnp.where(
                    mask, value, 0.0
                )

        tiles = []
        for tile in range(sticks.shape[0] // LANES):
            value = sticks[tile * LANES : (tile + 1) * LANES].T
            sums = []
            for part in range(2):
                terms = [
                    value[part * half + slot * bz : part * half + (slot + 1) * bz]
                    for slot in range(slots)
                ]
                sums.append(sum(terms[1:], terms[0]))
            tiles.append(jnp.concatenate(sums, axis=0))
        value = jnp.concatenate(tiles, axis=1)[:, :own]
        for part in range(2):
            for band in range(bands):
                start = (part * bands + band) * planes
                ready[
                    device, part * planes : (part + 1) * planes, band * own : (band + 1) * own
                ] = value[start : start + planes]

    sticks[...] = jnp.zeros_like(sticks)
    gather(peers.me)
    field[peers.me] = ready[peers.me]
    peers.met()

    @pl.loop(1, devices)
    def _(step):
        gather(peers.at(step))
        peers.copy(step, ready, field, sent, got).start()

    pw = pw_ref[...]
    first = lax.broadcasted_iota(jnp.int32, (rows, LANES), 1) < width // 2
    peers.settle(ready, field, sent, got)
    for device in range(devices):
        flat[device * part_rows : (device + 1) * part_rows] = field[device]
    column = dot3(split(flat[...]), (table_hi[...], table_lo[...]), ((0,), (0,)))
    for band in range(bands):
        for part in range(2):
            taken = []
            for parity in range(2):
                start = (band * 2 + parity) * rows
                piece = column[start : start + rows, part * length : (part + 1) * length]
                taken.append(
                    jnp.take_along_axis(piece, pw, axis=1, mode="promise_in_bounds")
                )
            out_ref[part, band] = jnp.where(first, taken[0], taken[1])


VM = pl.BlockSpec(memory_space=pltpu.VMEM)
SM = pl.BlockSpec(memory_space=pltpu.SMEM)
params = partial(pltpu.CompilerParams, vmem_limit_bytes=40 * 1024 * 1024)


def local(dpsi, stick_cols, pw_z, v_local, dv):
    devices = lax.axis_size("pencil") * lax.axis_size("tgroup")
    cores = lax.axis_size("tgroup")
    core = lax.axis_index("tgroup")
    length = math.isqrt(v_local.shape[1])
    planes = v_local.shape[0] // cores
    own = pw_z.shape[0] // cores
    zpw = pw_z.shape[1]
    bands = dpsi.shape[1]
    pairs = own // 2
    bz = bands * planes
    slots = LANES // (2 * bz)

    rows = lax.dynamic_slice_in_dim(pw_z, core * own, own, 0).reshape(pairs, 2 * zpw)
    coeff = dpsi.reshape(2, bands, pairs, 2 * zpw)

    depth = halves(depth_table(length, devices))
    up, down = [halves(table) for table in row_tables(length)]
    column = column_table(length, slots)
    back = halves(np.ascontiguousarray(column.T))
    column = halves(column)

    block = (devices, 2 * planes, bands * own)
    in_slots = length // slots * length
    padded = -(-own // LANES) * LANES
    field, potential = pl.pallas_call(
        depth_up,
        out_shape=[
            jax.ShapeDtypeStruct(block, F32),
            jax.ShapeDtypeStruct((length * planes, length), F32),
        ],
        in_specs=[VM] * 4 + [pl.BlockSpec(memory_space=pl.ANY)] * 2,
        out_specs=[VM, VM],
        scratch_shapes=[
            pltpu.VMEM(block, F32),
            pltpu.VMEM(v_local.shape, F32),
            pltpu.VMEM(v_local.shape, F32),
            pltpu.SemaphoreType.DMA((devices,)),
            pltpu.SemaphoreType.DMA((devices,)),
            pltpu.SemaphoreType.DMA((2,)),
        ],
        compiler_params=params(collective_id=0, has_side_effects=True),
    )(coeff, rows, *depth, v_local, dv)
    grid = pl.pallas_call(
        partial(plane_kernel, bands),
        out_shape=jax.ShapeDtypeStruct((in_slots, LANES), F32),
        in_specs=[SM] + [VM] * 10,
        out_specs=VM,
        scratch_shapes=[
            pltpu.VMEM((2 * bz, devices * own), F32),
            pltpu.VMEM((devices * own, LANES), F32),
        ],
        compiler_params=params(),
    )(stick_cols, field, potential, *up, *down, *column, *back)
    output = pl.pallas_call(
        depth_down,
        out_shape=jax.ShapeDtypeStruct(coeff.shape, F32),
        in_specs=[SM] + [VM] * 4,
        out_specs=VM,
        scratch_shapes=[
            pltpu.VMEM(block, F32),
            pltpu.VMEM(block, F32),
            pltpu.VMEM((padded, LANES), F32),
            pltpu.VMEM((2 * length, bands * own), F32),
            pltpu.SemaphoreType.DMA((devices,)),
            pltpu.SemaphoreType.DMA((devices,)),
        ],
        compiler_params=params(collective_id=1, has_side_effects=True),
    )(stick_cols, grid, rows, *depth)
    return output.reshape(dpsi.shape)


def solution(mesh):
    in_specs = (
        P(None, "pool", ("pencil", "tgroup")),
        P(),
        P("pencil", None),
        P("pencil", None),
        P("pencil", None),
    )
    out_specs = P(None, "pool", ("pencil", "tgroup"))
    return jax.shard_map(local, mesh=mesh, in_specs=in_specs, out_specs=out_specs, check_vma=False)
```

```python
from functools import partial
import math

import jax
import jax.numpy as jnp
import ml_dtypes
import numpy as np
from jax import lax
from jax.experimental import pallas as pl
from jax.experimental.pallas import tpu as pltpu
from jax.sharding import PartitionSpec as P

F32 = jnp.float32
BF16 = jnp.bfloat16
LANES = 128
GROUP = 32


def halves(table):
    hi = table.astype(ml_dtypes.bfloat16)
    lo = (table - hi.astype(np.float64)).astype(ml_dtypes.bfloat16)
    return jnp.asarray(hi), jnp.asarray(lo)


def split(value):
    hi = value.astype(BF16)
    lo = (value - hi.astype(F32)).astype(BF16)
    return hi, lo


def dot3(left, right, dims=((1,), (0,))):
    mul = lambda a, b: lax.dot_general(a, b, (dims, ((), ())), preferred_element_type=F32)
    return mul(left[0], right[0]) + (mul(left[0], right[1]) + mul(left[1], right[0]))


def waves(length):
    k = np.arange(length)
    angle = (k[:, None] * k[None, :] % length) * (2.0 * math.pi / length)
    return np.cos(angle) / math.sqrt(length), np.sin(angle) / math.sqrt(length)


def depth_table(length, devices):
    cos, sin = waves(length)
    planes = length // devices
    whole = np.stack([np.stack([cos, -sin], 1), np.stack([sin, cos], 1)])
    whole = whole.reshape(2, devices, planes, 2 * length)
    return whole.transpose(1, 0, 2, 3).reshape(2 * length, 2 * length)


def row_tables(length):
    cos, sin = waves(length)
    return np.concatenate([cos, sin]), np.concatenate([cos, -sin])


def column_table(length, slots):
    cos, sin = waves(length)
    whole = np.stack([np.stack([cos, -sin], 1), np.stack([sin, cos], 1)])
    whole = whole.reshape(2, length, 2, slots, length // slots)
    return whole.transpose(0, 1, 4, 2, 3).reshape(2 * length, 2 * length)


class Peers:
    def __init__(self):
        self.cores = lax.axis_size("tgroup")
        self.count = lax.axis_size("pencil") * self.cores
        self.me = lax.axis_index("pencil") * self.cores + lax.axis_index("tgroup")
        self.barrier = pltpu.get_barrier_semaphore()

    def at(self, step):
        return lax.rem(self.me + step, self.count)

    def step(self, turn):
        away = lax.div(turn, 2)
        return self.count // 2 + jnp.where(lax.rem(turn, 2) == 0, away, -away)

    def name(self, device):
        return {"pencil": lax.div(device, self.cores), "tgroup": lax.rem(device, self.cores)}

    def greet(self):
        @pl.loop(1, self.count)
        def _(step):
            pl.semaphore_signal(
                self.barrier,
                inc=1,
                device_id=self.name(self.at(step)),
                device_id_type=pl.DeviceIdType.MESH,
            )

    def met(self):
        pl.semaphore_wait(self.barrier, self.count - 1)

    def copy(self, step, source, target, sent, got):
        peer = self.at(step)
        return pltpu.make_async_remote_copy(
            src_ref=source.at[peer],
            dst_ref=target.at[self.me],
            send_sem=sent.at[step],
            recv_sem=got.at[step],
            device_id=self.name(peer),
            device_id_type=pl.DeviceIdType.MESH,
        )

    def settle(self, source, target, sent, got):
        @pl.loop(1, self.count)
        def _(step):
            self.copy(step, source, target, sent, got).wait()


def depth_up(
    coeff_ref,
    pw_ref,
    hi_ref,
    lo_ref,
    local_ref,
    change_ref,
    out_ref,
    weight_ref,
    ready,
    column,
    table_hi,
    table_lo,
    first,
    second,
    sent,
    got,
    loads,
):
    peers = Peers()
    peers.greet()
    pairs = zip((hi_ref, lo_ref, local_ref, change_ref), (table_hi, table_lo, first, second))
    fetch = [pltpu.make_async_copy(*pair, loads.at[i]) for i, pair in enumerate(pairs)]
    for copy in fetch:
        copy.start()
    _, bands, rows, width = coeff_ref.shape
    devices, part_rows, _ = out_ref.shape
    zpw = width // 2
    pw = pw_ref[...]
    z = lax.broadcasted_iota(jnp.int32, (rows, LANES), 1)
    for parity in range(2):
        source = jnp.full((rows, LANES), -1, jnp.int32)
        for k in range(parity * zpw, (parity + 1) * zpw):
            source = jnp.where(pw[:, k : k + 1] == z, k, source)
        found = source >= 0
        source = jnp.maximum(source, 0)
        for band in range(bands):
            places = pl.ds(band * 2 * rows + parity, rows, stride=2)
            for part in range(2):
                taken = jnp.take_along_axis(
                    coeff_ref[part, band], source, axis=1, mode="promise_in_bounds"
                )
                column[part, places, :] = jnp.where(found, taken, 0.0)
    fetch[0].wait()
    fetch[1].wait()
    value = jnp.concatenate([column[0], column[1]], axis=1)
    field = dot3((table_hi[...], table_lo[...]), split(value), ((1,), (1,)))
    for device in range(devices):
        ready[device] = field[device * part_rows : (device + 1) * part_rows]
    peers.met()

    @pl.loop(1, devices)
    def _(turn):
        peers.copy(peers.step(turn), ready, out_ref, sent, got).start()

    out_ref[peers.me] = ready[peers.me]
    fetch[2].wait()
    fetch[3].wait()
    planes = part_rows // 2
    core = lax.axis_index("tgroup")
    for x in range(weight_ref.shape[0] // planes):
        lanes = slice(x * LANES, (x + 1) * LANES)
        whole = first[:, lanes] + second[:, lanes]
        mine = whole[:planes]
        for other in range(1, peers.cores):
            mine = jnp.where(core == other, whole[other * planes : (other + 1) * planes], mine)
        weight_ref[x * planes : (x + 1) * planes] = mine
    peers.settle(ready, out_ref, sent, got)


def turn(value):
    half = value.shape[0] // 2
    return jnp.concatenate([-value[half:], value[:half]], axis=0)


def row_product(pair, table):
    length = table.shape[1] // 2
    mul = partial(jnp.dot, preferred_element_type=F32)
    both = mul(pair[0], table[...])
    return both[:, :length] + (both[:, length:] + mul(pair[1], table[:, :length]))


def plane_kernel(
    bands,
    cols_ref,
    field_ref,
    weight_ref,
    up,
    down,
    column_hi,
    column_lo,
    back_hi,
    back_lo,
    out_ref,
    flat,
    sticks,
    grid,
    other,
):
    devices, part_rows, block = field_ref.shape
    planes = part_rows // 2
    own = block // bands
    length = weight_ref.shape[1]
    bz = bands * planes
    slots = LANES // (2 * bz)
    inner = length // slots
    group_rows = inner * length
    batch = math.gcd(inner, 8)
    total = devices * own
    shift = group_rows.bit_length() - 1

    grid[...] = jnp.zeros_like(grid)
    for device in range(devices):
        for part in range(2):
            for band in range(bands):
                flat[
                    (part * bands + band) * planes : (part * bands + band + 1) * planes,
                    device * own : (device + 1) * own,
                ] = field_ref[
                    device, part * planes : (part + 1) * planes, band * own : (band + 1) * own
                ]
    for tile in range(total // LANES):
        value = flat[:, tile * LANES : (tile + 1) * LANES]
        value = jnp.concatenate([value[:bz]] * slots + [value[bz:]] * slots, axis=0)
        sticks[tile * LANES : (tile + 1) * LANES] = value.T

    lane = lax.broadcasted_iota(jnp.int32, (1, LANES), 1)
    slot_of_lane = lane // bz % slots

    @pl.loop(0, total // GROUP)
    def _(step):
        base = pl.multiple_of(step * GROUP, GROUP)
        cols = [cols_ref[base + i] for i in range(GROUP)]
        rows = [col & (group_rows - 1) for col in cols]
        masks = [slot_of_lane == lax.shift_right_logical(col, shift) for col in cols]
        values = [sticks[pl.ds(base + i, 1), :] for i in range(GROUP)]
        for value, row, mask in zip(values, rows, masks):
            pltpu.store(grid.at[pl.ds(row, 1), :], value, mask=mask)

    @pl.loop(0, inner // batch)
    def _(step):
        whole = pl.ds(pl.multiple_of(step * batch * length, batch * length), batch * length)
        his, los = [], []
        for i in range(batch):
            start = pl.multiple_of((step * batch + i) * length, length)
            hi, lo = split(grid[pl.ds(start, length), :].T)
            his.append(jnp.concatenate([hi, turn(hi)], axis=1))
            los.append(jnp.concatenate([lo, turn(lo)], axis=1))
        pair = (jnp.concatenate(his, axis=0), jnp.concatenate(los, axis=0))
        other[whole, :] = row_product(pair, up)

    for z in range(planes):
        picks = [pl.ds(band * planes + z, 2 * length, stride=bz) for band in range(bands)]
        value = jnp.concatenate([other[pick, :] for pick in picks], axis=1)
        value = dot3((column_hi[...], column_lo[...]), split(value))
        weight = weight_ref[pl.ds(z, length, stride=planes), :]
        weight = jnp.concatenate([weight] * 2, axis=0)
        weight = jnp.concatenate([weight] * bands, axis=1)
        value = dot3((back_hi[...], back_lo[...]), split(value * weight))
        for band, pick in enumerate(picks):
            grid[pick, :] = value[:, band * length : (band + 1) * length]

    @pl.loop(0, inner // batch)
    def _(step):
        his, los = [], []
        starts = [pl.multiple_of((step * batch + i) * length, length) for i in range(batch)]
        for start in starts:
            hi, lo = split(grid[pl.ds(start, length), :])
            his.append(jnp.concatenate([hi, turn(hi)], axis=1))
            los.append(jnp.concatenate([lo, turn(lo)], axis=1))
        pair = (jnp.concatenate(his, axis=0), jnp.concatenate(los, axis=0))
        value = row_product(pair, down)
        for i, start in enumerate(starts):
            out_ref[pl.ds(start, length), :] = value[i * length : (i + 1) * length].T


def depth_down(
    cols_ref,
    slot_ref,
    grid_ref,
    pw_ref,
    table_hi,
    table_lo,
    out_ref,
    ready,
    field,
    sticks,
    flat,
    column,
    sent,
    got,
):
    peers = Peers()
    peers.greet()
    _, bands, rows, width = out_ref.shape
    devices, part_rows, _ = ready.shape
    planes = part_rows // 2
    own = 2 * rows
    length = devices * planes
    bz = bands * planes
    slots = LANES // (2 * bz)
    half = slots * bz
    group_rows = grid_ref.shape[0]
    shift = group_rows.bit_length() - 1
    group = math.gcd(own, GROUP)

    def gather(device):
        @pl.loop(0, own // group)
        def _(chunk):
            start = pl.multiple_of(chunk * group, group)
            first = device * own + start
            cols = [cols_ref[first + i] for i in range(group)]
            values = [grid_ref[pl.ds(col & (group_rows - 1), 1), :] for col in cols]
            for i, value in enumerate(values):
                sticks[pl.ds(start + i, 1), :] = value

        slot_of = lax.shift_right_logical(slot_ref[device], shift)

        tiles = []
        for tile in range(sticks.shape[0] // LANES):
            value = sticks[tile * LANES : (tile + 1) * LANES].T
            here = slot_of[:, tile * LANES : (tile + 1) * LANES]
            sums = []
            for part in range(2):
                total = value[part * half : part * half + bz]
                for slot in range(1, slots):
                    start = part * half + slot * bz
                    total = jnp.where(here == slot, value[start : start + bz], total)
                sums.append(total)
            tiles.append(jnp.concatenate(sums, axis=0))
        value = jnp.concatenate(tiles, axis=1)[:, :own]
        for part in range(2):
            for band in range(bands):
                start = (part * bands + band) * planes
                ready[
                    device, part * planes : (part + 1) * planes, band * own : (band + 1) * own
                ] = value[start : start + planes]

    sticks[...] = jnp.zeros_like(sticks)
    gather(peers.me)
    field[peers.me] = ready[peers.me]
    peers.met()

    @pl.loop(1, devices)
    def _(turn):
        step = peers.step(turn)
        gather(peers.at(step))
        peers.copy(step, ready, field, sent, got).start()

    pw = pw_ref[...]
    first = lax.broadcasted_iota(jnp.int32, (rows, LANES), 1) < width // 2
    peers.settle(ready, field, sent, got)
    for device in range(devices):
        flat[device * part_rows : (device + 1) * part_rows] = field[device]
    value = dot3(split(flat[...]), (table_hi[...], table_lo[...]), ((0,), (0,)))
    column[0] = value[:, :length]
    column[1] = value[:, length:]
    for band in range(bands):
        for part in range(2):
            taken = []
            for parity in range(2):
                piece = column[part, pl.ds(band * own + parity, rows, stride=2), :]
                taken.append(
                    jnp.take_along_axis(piece, pw, axis=1, mode="promise_in_bounds")
                )
            out_ref[part, band] = jnp.where(first, taken[0], taken[1])


VM = pl.BlockSpec(memory_space=pltpu.VMEM)
SM = pl.BlockSpec(memory_space=pltpu.SMEM)
params = partial(pltpu.CompilerParams, vmem_limit_bytes=40 * 1024 * 1024)


def local(dpsi, stick_cols, pw_z, v_local, dv):
    devices = lax.axis_size("pencil") * lax.axis_size("tgroup")
    cores = lax.axis_size("tgroup")
    core = lax.axis_index("tgroup")
    length = math.isqrt(v_local.shape[1])
    planes = v_local.shape[0] // cores
    own = pw_z.shape[0] // cores
    zpw = pw_z.shape[1]
    bands = dpsi.shape[1]
    pairs = own // 2
    bz = bands * planes
    slots = LANES // (2 * bz)

    rows = lax.dynamic_slice_in_dim(pw_z, core * own, own, 0).reshape(pairs, 2 * zpw)
    coeff = dpsi.reshape(2, bands, pairs, 2 * zpw)

    depth = halves(depth_table(length, devices))
    up, down = [jnp.concatenate(halves(table), axis=1) for table in row_tables(length)]
    column = column_table(length, slots)
    back = halves(np.ascontiguousarray(column.T))
    column = halves(column)

    slot_cols = jnp.pad(stick_cols.reshape(devices, 1, own), ((0, 0), (0, 0), (0, -own % LANES)))
    block = (devices, 2 * planes, bands * own)
    in_slots = length // slots * length
    padded = -(-own // LANES) * LANES
    field, potential = pl.pallas_call(
        depth_up,
        out_shape=[
            jax.ShapeDtypeStruct(block, F32),
            jax.ShapeDtypeStruct((length * planes, length), F32),
        ],
        in_specs=[VM] * 2 + [pl.BlockSpec(memory_space=pltpu.HBM)] * 4,
        out_specs=[VM, VM],
        scratch_shapes=[
            pltpu.VMEM(block, F32),
            pltpu.VMEM((2, bands * own, length), F32),
            pltpu.VMEM(depth[0].shape, BF16),
            pltpu.VMEM(depth[1].shape, BF16),
            pltpu.VMEM(v_local.shape, F32),
            pltpu.VMEM(v_local.shape, F32),
            pltpu.SemaphoreType.DMA((devices,)),
            pltpu.SemaphoreType.DMA((devices,)),
            pltpu.SemaphoreType.DMA((4,)),
        ],
        compiler_params=params(collective_id=0, has_side_effects=True),
    )(coeff, rows, *depth, v_local, dv)
    grid = pl.pallas_call(
        partial(plane_kernel, bands),
        out_shape=jax.ShapeDtypeStruct((in_slots, LANES), F32),
        in_specs=[SM] + [VM] * 8,
        out_specs=VM,
        scratch_shapes=[
            pltpu.VMEM((2 * bz, devices * own), F32),
            pltpu.VMEM((devices * own, LANES), F32),
            pltpu.VMEM((in_slots, LANES), F32),
            pltpu.VMEM((in_slots, LANES), F32),
        ],
        compiler_params=params(),
    )(stick_cols, field, potential, up, down, *column, *back)
    output = pl.pallas_call(
        depth_down,
        out_shape=jax.ShapeDtypeStruct(coeff.shape, F32),
        in_specs=[SM] + [VM] * 5,
        out_specs=VM,
        scratch_shapes=[
            pltpu.VMEM(block, F32),
            pltpu.VMEM(block, F32),
            pltpu.VMEM((padded, LANES), F32),
            pltpu.VMEM((2 * length, bands * own), F32),
            pltpu.VMEM((2, bands * own, length), F32),
            pltpu.SemaphoreType.DMA((devices,)),
            pltpu.SemaphoreType.DMA((devices,)),
        ],
        compiler_params=params(collective_id=1, has_side_effects=True),
    )(stick_cols, slot_cols, grid, rows, *depth)
    return output.reshape(dpsi.shape)


def solution(mesh):
    in_specs = (
        P(None, "pool", ("pencil", "tgroup")),
        P(),
        P("pencil", None),
        P("pencil", None),
        P("pencil", None),
    )
    out_specs = P(None, "pool", ("pencil", "tgroup"))
    return jax.shard_map(local, mesh=mesh, in_specs=in_specs, out_specs=out_specs, check_vma=False)
```

```python
from functools import partial
import math

import jax
import jax.numpy as jnp
import ml_dtypes
import numpy as np
from jax import lax
from jax.experimental import pallas as pl
from jax.experimental.pallas import tpu as pltpu
from jax.sharding import PartitionSpec as P

F32 = jnp.float32
BF16 = jnp.bfloat16
LANES = 128
GROUP = 32


def halves(table):
    hi = table.astype(ml_dtypes.bfloat16)
    lo = (table - hi.astype(np.float64)).astype(ml_dtypes.bfloat16)
    return hi, lo


def split(value):
    hi = value.astype(BF16)
    lo = (value - hi.astype(F32)).astype(BF16)
    return hi, lo


def dot3(left, right, dims=((1,), (0,))):
    mul = lambda a, b: lax.dot_general(a, b, (dims, ((), ())), preferred_element_type=F32)
    return mul(left[0], right[0]) + (mul(left[0], right[1]) + mul(left[1], right[0]))


def waves(length):
    k = np.arange(length)
    angle = (k[:, None] * k[None, :] % length) * (2.0 * math.pi / length)
    return np.cos(angle) / math.sqrt(length), np.sin(angle) / math.sqrt(length)


def depth_table(length, devices):
    cos, sin = waves(length)
    planes = length // devices
    whole = np.stack([np.stack([cos, -sin], 1), np.stack([sin, cos], 1)])
    whole = whole.reshape(2, devices, planes, 2 * length)
    return whole.transpose(1, 0, 2, 3).reshape(2 * length, 2 * length)


def row_tables(length):
    cos, sin = waves(length)
    return np.concatenate([cos, sin]), np.concatenate([cos, -sin])


def column_table(length, slots):
    cos, sin = waves(length)
    whole = np.stack([np.stack([cos, -sin], 1), np.stack([sin, cos], 1)])
    whole = whole.reshape(2, length, 2, slots, length // slots)
    return whole.transpose(0, 1, 4, 2, 3).reshape(2 * length, 2 * length)


class Peers:
    def __init__(self):
        self.cores = lax.axis_size("tgroup")
        self.count = lax.axis_size("pencil") * self.cores
        self.me = lax.axis_index("pencil") * self.cores + lax.axis_index("tgroup")
        self.barrier = pltpu.get_barrier_semaphore()

    def at(self, step):
        return lax.rem(self.me + step, self.count)

    def step(self, turn):
        away = lax.div(turn, 2)
        return self.count // 2 + jnp.where(lax.rem(turn, 2) == 0, away, -away)

    def name(self, device):
        return {"pencil": lax.div(device, self.cores), "tgroup": lax.rem(device, self.cores)}

    def greet(self):
        @pl.loop(1, self.count)
        def _(step):
            pl.semaphore_signal(
                self.barrier,
                inc=1,
                device_id=self.name(self.at(step)),
                device_id_type=pl.DeviceIdType.MESH,
            )

    def met(self):
        pl.semaphore_wait(self.barrier, self.count - 1)

    def copy(self, step, source, target, sent, got):
        peer = self.at(step)
        return pltpu.make_async_remote_copy(
            src_ref=source.at[peer],
            dst_ref=target.at[self.me],
            send_sem=sent.at[step],
            recv_sem=got.at[step],
            device_id=self.name(peer),
            device_id_type=pl.DeviceIdType.MESH,
        )

    def settle(self, source, target, sent, got):
        @pl.loop(1, self.count)
        def _(step):
            self.copy(step, source, target, sent, got).wait()


def depth_up(
    coeff_ref,
    pw_ref,
    table_ref,
    out_ref,
    ready,
    coeff,
    inverse,
    column,
    sent,
    got,
):
    peers = Peers()
    peers.greet()
    bands = coeff_ref.shape[1]
    _, _, rows, width = coeff.shape
    devices, part_rows, _ = out_ref.shape
    zpw, own = pw_ref.shape
    length = inverse.shape[1]
    for part in range(2):
        for band in range(bands):
            for row in range(rows):
                coeff[part, band, row : row + 1] = coeff_ref[
                    part, band : band + 1, row * width : (row + 1) * width
                ]
    z = lax.broadcasted_iota(jnp.int32, (length, LANES), 0)
    for tile in range(own // LANES + (own % LANES > 0)):
        lanes = slice(tile * LANES, min((tile + 1) * LANES, own))
        source = jnp.full((length, LANES), -1, jnp.int32)
        for k in range(zpw):
            row = pw_ref[k : k + 1, lanes]
            if row.shape[1] < LANES:
                row = jnp.concatenate(
                    [row, jnp.full((1, LANES - row.shape[1]), -1, jnp.int32)], axis=1
                )
            source = jnp.where(row == z, k, source)
        inverse[tile * LANES : (tile + 1) * LANES] = source.T
    for parity in range(2):
        source = inverse[pl.ds(parity, rows, stride=2), :]
        found = source >= 0
        source = jnp.maximum(source, 0) + parity * zpw
        for band in range(bands):
            places = pl.ds(band * own + parity, rows, stride=2)
            for part in range(2):
                taken = jnp.take_along_axis(
                    coeff[part, band], source, axis=1, mode="promise_in_bounds"
                )
                column[part, places, :] = jnp.where(found, taken, 0.0)
    value = jnp.concatenate([column[0], column[1]], axis=1)
    field = dot3((table_ref[0], table_ref[1]), split(value), ((1,), (1,)))
    for device in range(devices):
        ready[device] = field[device * part_rows : (device + 1) * part_rows]
    peers.met()

    @pl.loop(1, devices)
    def _(turn):
        peers.copy(peers.step(turn), ready, out_ref, sent, got).start()

    out_ref[peers.me] = ready[peers.me]
    peers.settle(ready, out_ref, sent, got)


def turn(value):
    half = value.shape[0] // 2
    return jnp.concatenate([-value[half:], value[:half]], axis=0)


def row_product(pair, table):
    length = table.shape[1] // 2
    mul = partial(jnp.dot, preferred_element_type=F32)
    both = mul(pair[0], table[...])
    return both[:, :length] + (both[:, length:] + mul(pair[1], table[:, :length]))


def plane_kernel(
    bands,
    cols_ref,
    field_ref,
    local_ref,
    change_ref,
    up,
    down,
    column_hi,
    column_lo,
    back_hi,
    back_lo,
    out_ref,
    flat,
    sticks,
    grid,
    other,
    weights,
):
    devices, part_rows, block = field_ref.shape
    planes = part_rows // 2
    own = block // bands
    length = math.isqrt(local_ref.shape[1])
    bz = bands * planes
    slots = LANES // (2 * bz)
    inner = length // slots
    group_rows = inner * length
    batch = math.gcd(inner, 8)
    total = devices * own
    shift = group_rows.bit_length() - 1

    core = lax.axis_index("tgroup")
    for x in range(length):
        lanes = slice(x * length, (x + 1) * length)
        whole = local_ref[:, lanes] + change_ref[:, lanes]
        mine = whole[:planes]
        for rank in range(1, lax.axis_size("tgroup")):
            mine = jnp.where(core == rank, whole[rank * planes : (rank + 1) * planes], mine)
        weights[x * planes : (x + 1) * planes] = mine
    grid[...] = jnp.zeros_like(grid)
    for device in range(devices):
        for part in range(2):
            for band in range(bands):
                flat[
                    (part * bands + band) * planes : (part * bands + band + 1) * planes,
                    device * own : (device + 1) * own,
                ] = field_ref[
                    device, part * planes : (part + 1) * planes, band * own : (band + 1) * own
                ]
    for tile in range(total // LANES):
        value = flat[:, tile * LANES : (tile + 1) * LANES]
        value = jnp.concatenate([value[:bz]] * slots + [value[bz:]] * slots, axis=0)
        sticks[tile * LANES : (tile + 1) * LANES] = value.T

    lane = lax.broadcasted_iota(jnp.int32, (1, LANES), 1)
    slot_of_lane = lane // bz % slots

    @pl.loop(0, total // GROUP)
    def _(step):
        base = pl.multiple_of(step * GROUP, GROUP)
        cols = [cols_ref[base + i] for i in range(GROUP)]
        rows = [col & (group_rows - 1) for col in cols]
        masks = [slot_of_lane == lax.shift_right_logical(col, shift) for col in cols]
        values = [sticks[pl.ds(base + i, 1), :] for i in range(GROUP)]
        for value, row, mask in zip(values, rows, masks):
            pltpu.store(grid.at[pl.ds(row, 1), :], value, mask=mask)

    @pl.loop(0, inner // batch)
    def _(step):
        whole = pl.ds(pl.multiple_of(step * batch * length, batch * length), batch * length)
        his, los = [], []
        for i in range(batch):
            start = pl.multiple_of((step * batch + i) * length, length)
            hi, lo = split(grid[pl.ds(start, length), :].T)
            his.append(jnp.concatenate([hi, turn(hi)], axis=1))
            los.append(jnp.concatenate([lo, turn(lo)], axis=1))
        pair = (jnp.concatenate(his, axis=0), jnp.concatenate(los, axis=0))
        other[whole, :] = row_product(pair, up)

    for z in range(planes):
        picks = [pl.ds(band * planes + z, 2 * length, stride=bz) for band in range(bands)]
        value = jnp.concatenate([other[pick, :] for pick in picks], axis=1)
        value = dot3((column_hi[...], column_lo[...]), split(value))
        weight = weights[pl.ds(z, length, stride=planes), :]
        weight = jnp.concatenate([weight] * 2, axis=0)
        weight = jnp.concatenate([weight] * bands, axis=1)
        value = dot3((back_hi[...], back_lo[...]), split(value * weight))
        for band, pick in enumerate(picks):
            grid[pick, :] = value[:, band * length : (band + 1) * length]

    @pl.loop(0, inner // batch)
    def _(step):
        his, los = [], []
        starts = [pl.multiple_of((step * batch + i) * length, length) for i in range(batch)]
        for start in starts:
            hi, lo = split(grid[pl.ds(start, length), :])
            his.append(jnp.concatenate([hi, turn(hi)], axis=1))
            los.append(jnp.concatenate([lo, turn(lo)], axis=1))
        pair = (jnp.concatenate(his, axis=0), jnp.concatenate(los, axis=0))
        value = row_product(pair, down)
        for i, start in enumerate(starts):
            out_ref[pl.ds(start, length), :] = value[i * length : (i + 1) * length].T


def depth_down(
    cols_ref,
    slot_ref,
    grid_ref,
    pw_ref,
    table_ref,
    out_ref,
    ready,
    field,
    sticks,
    flat,
    column,
    sent,
    got,
):
    peers = Peers()
    peers.greet()
    _, bands, rows, width = out_ref.shape
    devices, part_rows, _ = ready.shape
    planes = part_rows // 2
    own = 2 * rows
    length = devices * planes
    bz = bands * planes
    slots = LANES // (2 * bz)
    half = slots * bz
    group_rows = grid_ref.shape[0]
    shift = group_rows.bit_length() - 1
    group = math.gcd(own, GROUP)

    def gather(device):
        @pl.loop(0, own // group)
        def _(chunk):
            start = pl.multiple_of(chunk * group, group)
            first = device * own + start
            cols = [cols_ref[first + i] for i in range(group)]
            values = [grid_ref[pl.ds(col & (group_rows - 1), 1), :] for col in cols]
            for i, value in enumerate(values):
                sticks[pl.ds(start + i, 1), :] = value

        slot_of = lax.shift_right_logical(slot_ref[device], shift)

        tiles = []
        for tile in range(sticks.shape[0] // LANES):
            value = sticks[tile * LANES : (tile + 1) * LANES].T
            here = slot_of[:, tile * LANES : (tile + 1) * LANES]
            sums = []
            for part in range(2):
                total = value[part * half : part * half + bz]
                for slot in range(1, slots):
                    start = part * half + slot * bz
                    total = jnp.where(here == slot, value[start : start + bz], total)
                sums.append(total)
            tiles.append(jnp.concatenate(sums, axis=0))
        value = jnp.concatenate(tiles, axis=1)[:, :own]
        for part in range(2):
            for band in range(bands):
                start = (part * bands + band) * planes
                ready[
                    device, part * planes : (part + 1) * planes, band * own : (band + 1) * own
                ] = value[start : start + planes]

    sticks[...] = jnp.zeros_like(sticks)
    gather(peers.at(peers.step(1)))
    peers.met()
    peers.copy(peers.step(1), ready, field, sent, got).start()

    @pl.loop(2, devices)
    def _(turn):
        step = peers.step(turn)
        gather(peers.at(step))
        peers.copy(step, ready, field, sent, got).start()

    gather(peers.me)
    field[peers.me] = ready[peers.me]
    pw = pw_ref[...]
    first = lax.broadcasted_iota(jnp.int32, (rows, LANES), 1) < width // 2
    peers.settle(ready, field, sent, got)
    for device in range(devices):
        flat[device * part_rows : (device + 1) * part_rows] = field[device]
    value = dot3(split(flat[...]), (table_ref[0], table_ref[1]), ((0,), (0,)))
    column[0] = value[:, :length]
    column[1] = value[:, length:]
    for band in range(bands):
        for part in range(2):
            taken = []
            for parity in range(2):
                piece = column[part, pl.ds(band * own + parity, rows, stride=2), :]
                taken.append(
                    jnp.take_along_axis(piece, pw, axis=1, mode="promise_in_bounds")
                )
            out_ref[part, band] = jnp.where(first, taken[0], taken[1])


VM = pl.BlockSpec(memory_space=pltpu.VMEM)
SM = pl.BlockSpec(memory_space=pltpu.SMEM)
params = partial(pltpu.CompilerParams, vmem_limit_bytes=40 * 1024 * 1024)


def local(dpsi, stick_cols, pw_z, v_local, dv):
    devices = lax.axis_size("pencil") * lax.axis_size("tgroup")
    cores = lax.axis_size("tgroup")
    core = lax.axis_index("tgroup")
    length = math.isqrt(v_local.shape[1])
    planes = v_local.shape[0] // cores
    own = pw_z.shape[0] // cores
    zpw = pw_z.shape[1]
    bands = dpsi.shape[1]
    pairs = own // 2
    bz = bands * planes
    slots = LANES // (2 * bz)

    rows = lax.dynamic_slice_in_dim(pw_z, core * own, own, 0).reshape(pairs, 2 * zpw)
    coeff = (2, bands, pairs, 2 * zpw)
    by_wave = lax.dynamic_slice_in_dim(pw_z.T, core * own, own, 1)

    depth = jnp.asarray(np.stack(halves(depth_table(length, devices))))
    up, down = [jnp.asarray(np.concatenate(halves(table), axis=1)) for table in row_tables(length)]
    column = column_table(length, slots)
    back = [jnp.asarray(half) for half in halves(np.ascontiguousarray(column.T))]
    column = [jnp.asarray(half) for half in halves(column)]

    slot_cols = jnp.pad(stick_cols.reshape(devices, 1, own), ((0, 0), (0, 0), (0, -own % LANES)))
    block = (devices, 2 * planes, bands * own)
    in_slots = length // slots * length
    padded = -(-own // LANES) * LANES
    field = pl.pallas_call(
        depth_up,
        out_shape=jax.ShapeDtypeStruct(block, F32),
        in_specs=[VM] * 3,
        out_specs=VM,
        scratch_shapes=[
            pltpu.VMEM(block, F32),
            pltpu.VMEM(coeff, F32),
            pltpu.VMEM((padded, length), jnp.int32),
            pltpu.VMEM((2, bands * own, length), F32),
            pltpu.SemaphoreType.DMA((devices,)),
            pltpu.SemaphoreType.DMA((devices,)),
        ],
        compiler_params=params(collective_id=0, has_side_effects=True),
    )(dpsi, by_wave, depth)
    grid = pl.pallas_call(
        partial(plane_kernel, bands),
        out_shape=jax.ShapeDtypeStruct((in_slots, LANES), F32),
        in_specs=[SM] + [VM] * 9,
        out_specs=VM,
        scratch_shapes=[
            pltpu.VMEM((2 * bz, devices * own), F32),
            pltpu.VMEM((devices * own, LANES), F32),
            pltpu.VMEM((in_slots, LANES), F32),
            pltpu.VMEM((in_slots, LANES), F32),
            pltpu.VMEM((length * planes, length), F32),
        ],
        compiler_params=params(),
    )(stick_cols, field, v_local, dv, up, down, *column, *back)
    output = pl.pallas_call(
        depth_down,
        out_shape=jax.ShapeDtypeStruct(coeff, F32),
        in_specs=[SM] + [VM] * 4,
        out_specs=VM,
        scratch_shapes=[
            pltpu.VMEM(block, F32),
            pltpu.VMEM(block, F32),
            pltpu.VMEM((padded, LANES), F32),
            pltpu.VMEM((2 * length, bands * own), F32),
            pltpu.VMEM((2, bands * own, length), F32),
            pltpu.SemaphoreType.DMA((devices,)),
            pltpu.SemaphoreType.DMA((devices,)),
        ],
        compiler_params=params(collective_id=1, has_side_effects=True),
    )(stick_cols, slot_cols, grid, rows, depth)
    return output.reshape(dpsi.shape)


def solution(mesh):
    in_specs = (
        P(None, "pool", ("pencil", "tgroup")),
        P(),
        P("pencil", None),
        P("pencil", None),
        P("pencil", None),
    )
    out_specs = P(None, "pool", ("pencil", "tgroup"))
    return jax.shard_map(local, mesh=mesh, in_specs=in_specs, out_specs=out_specs, check_vma=False)
```

```python
from functools import partial
import math

import jax
import jax.numpy as jnp
import ml_dtypes
import numpy as np
from jax import lax
from jax.experimental import pallas as pl
from jax.experimental.pallas import tpu as pltpu
from jax.sharding import PartitionSpec as P

F32 = jnp.float32
BF16 = jnp.bfloat16
LANES = 128
GROUP = 32


def halves(table):
    hi = table.astype(ml_dtypes.bfloat16)
    lo = (table - hi.astype(np.float64)).astype(ml_dtypes.bfloat16)
    return hi, lo


def split(value):
    hi = value.astype(BF16)
    lo = (value - hi.astype(F32)).astype(BF16)
    return hi, lo


def dot3(left, right, dims=((1,), (0,))):
    mul = lambda a, b: lax.dot_general(a, b, (dims, ((), ())), preferred_element_type=F32)
    return mul(left[0], right[0]) + (mul(left[0], right[1]) + mul(left[1], right[0]))


def waves(length):
    k = np.arange(length)
    angle = (k[:, None] * k[None, :] % length) * (2.0 * math.pi / length)
    return np.cos(angle) / math.sqrt(length), np.sin(angle) / math.sqrt(length)


def depth_table(length, devices):
    cos, sin = waves(length)
    planes = length // devices
    whole = np.stack([np.stack([cos, -sin], 1), np.stack([sin, cos], 1)])
    whole = whole.reshape(2, devices, planes, 2 * length)
    return whole.transpose(1, 0, 2, 3).reshape(2 * length, 2 * length)


def row_tables(length):
    cos, sin = waves(length)
    return np.concatenate([cos, sin]), np.concatenate([cos, -sin])


def column_table(length, slots):
    cos, sin = waves(length)
    whole = np.stack([np.stack([cos, -sin], 1), np.stack([sin, cos], 1)])
    whole = whole.reshape(2, length, 2, slots, length // slots)
    return whole.transpose(0, 1, 4, 2, 3).reshape(2 * length, 2 * length)


class Peers:
    def __init__(self):
        self.cores = lax.axis_size("tgroup")
        self.count = lax.axis_size("pencil") * self.cores
        self.me = lax.axis_index("pencil") * self.cores + lax.axis_index("tgroup")
        self.barrier = pltpu.get_barrier_semaphore()

    def at(self, step):
        return lax.rem(self.me + step, self.count)

    def step(self, turn):
        away = lax.div(turn, 2)
        return self.count // 2 + jnp.where(lax.rem(turn, 2) == 0, away, -away)

    def name(self, device):
        return {"pencil": lax.div(device, self.cores), "tgroup": lax.rem(device, self.cores)}

    def greet(self):
        @pl.loop(1, self.count)
        def _(step):
            pl.semaphore_signal(
                self.barrier,
                inc=1,
                device_id=self.name(self.at(step)),
                device_id_type=pl.DeviceIdType.MESH,
            )

    def met(self):
        pl.semaphore_wait(self.barrier, self.count - 1)

    def copy(self, step, source, target, sent, got):
        peer = self.at(step)
        return pltpu.make_async_remote_copy(
            src_ref=source.at[peer],
            dst_ref=target.at[self.me],
            send_sem=sent.at[step],
            recv_sem=got.at[step],
            device_id=self.name(peer),
            device_id_type=pl.DeviceIdType.MESH,
        )

    def settle(self, source, target, sent, got):
        @pl.loop(1, self.count)
        def _(step):
            self.copy(step, source, target, sent, got).wait()


def depth_up(
    coeff_ref,
    pw_ref,
    table_ref,
    out_ref,
    ready,
    coeff,
    inverse,
    column,
    sent,
    got,
):
    peers = Peers()
    peers.greet()
    bands = coeff_ref.shape[1]
    _, _, rows, width = coeff.shape
    devices, part_rows, _ = out_ref.shape
    zpw, own = pw_ref.shape
    length = inverse.shape[1]
    for part in range(2):
        for band in range(bands):
            for row in range(rows):
                coeff[part, band, row : row + 1] = coeff_ref[
                    part, band : band + 1, row * width : (row + 1) * width
                ]
    z = lax.broadcasted_iota(jnp.int32, (length, LANES), 0)
    for tile in range(own // LANES + (own % LANES > 0)):
        lanes = slice(tile * LANES, min((tile + 1) * LANES, own))
        source = jnp.full((length, LANES), -1, jnp.int32)
        for k in range(zpw):
            row = pw_ref[k : k + 1, lanes]
            if row.shape[1] < LANES:
                row = jnp.concatenate(
                    [row, jnp.full((1, LANES - row.shape[1]), -1, jnp.int32)], axis=1
                )
            source = jnp.where(row == z, k, source)
        inverse[tile * LANES : (tile + 1) * LANES] = source.T
    for parity in range(2):
        source = inverse[pl.ds(parity, rows, stride=2), :]
        found = source >= 0
        source = jnp.maximum(source, 0) + parity * zpw
        for band in range(bands):
            places = pl.ds(band * own + parity, rows, stride=2)
            for part in range(2):
                taken = jnp.take_along_axis(
                    coeff[part, band], source, axis=1, mode="promise_in_bounds"
                )
                column[part, places, :] = jnp.where(found, taken, 0.0)
    value = jnp.concatenate([column[0], column[1]], axis=1)
    field = dot3((table_ref[0], table_ref[1]), split(value), ((1,), (1,)))
    for device in range(devices):
        ready[device] = field[device * part_rows : (device + 1) * part_rows]
    peers.met()

    @pl.loop(1, devices)
    def _(turn):
        peers.copy(peers.step(turn), ready, out_ref, sent, got).start()

    out_ref[peers.me] = ready[peers.me]
    peers.settle(ready, out_ref, sent, got)


def turn(value):
    half = value.shape[0] // 2
    return jnp.concatenate([-value[half:], value[:half]], axis=0)


def row_product(pair, table):
    length = table.shape[1] // 2
    mul = partial(jnp.dot, preferred_element_type=F32)
    both = mul(pair[0], table[...])
    return both[:, :length] + (both[:, length:] + mul(pair[1], table[:, :length]))


def plane_kernel(
    bands,
    cols_ref,
    field_ref,
    local_ref,
    change_ref,
    up,
    down,
    column_hi,
    column_lo,
    back_hi,
    back_lo,
    out_ref,
    flat,
    sticks,
    grid,
    other,
    weights,
):
    devices, part_rows, block = field_ref.shape
    planes = part_rows // 2
    own = block // bands
    length = math.isqrt(local_ref.shape[1])
    bz = bands * planes
    slots = LANES // (2 * bz)
    inner = length // slots
    group_rows = inner * length
    batch = math.gcd(inner, 8)
    total = devices * own
    shift = group_rows.bit_length() - 1

    core = lax.axis_index("tgroup")
    for x in range(length):
        lanes = slice(x * length, (x + 1) * length)
        whole = local_ref[:, lanes] + change_ref[:, lanes]
        mine = whole[:planes]
        for rank in range(1, lax.axis_size("tgroup")):
            mine = jnp.where(core == rank, whole[rank * planes : (rank + 1) * planes], mine)
        weights[x * planes : (x + 1) * planes] = mine
    grid[...] = jnp.zeros_like(grid)
    for device in range(devices):
        for part in range(2):
            for band in range(bands):
                flat[
                    (part * bands + band) * planes : (part * bands + band + 1) * planes,
                    device * own : (device + 1) * own,
                ] = field_ref[
                    device, part * planes : (part + 1) * planes, band * own : (band + 1) * own
                ]
    for tile in range(total // LANES):
        value = flat[:, tile * LANES : (tile + 1) * LANES]
        value = jnp.concatenate([value[:bz]] * slots + [value[bz:]] * slots, axis=0)
        sticks[tile * LANES : (tile + 1) * LANES] = value.T

    lane = lax.broadcasted_iota(jnp.int32, (1, LANES), 1)
    slot_of_lane = lane // bz % slots

    @pl.loop(0, total // GROUP)
    def _(step):
        base = pl.multiple_of(step * GROUP, GROUP)
        cols = [cols_ref[base + i] for i in range(GROUP)]
        rows = [col & (group_rows - 1) for col in cols]
        masks = [slot_of_lane == lax.shift_right_logical(col, shift) for col in cols]
        values = [sticks[pl.ds(base + i, 1), :] for i in range(GROUP)]
        for value, row, mask in zip(values, rows, masks):
            pltpu.store(grid.at[pl.ds(row, 1), :], value, mask=mask)

    @pl.loop(0, inner // batch)
    def _(step):
        whole = pl.ds(pl.multiple_of(step * batch * length, batch * length), batch * length)
        his, los = [], []
        for i in range(batch):
            start = pl.multiple_of((step * batch + i) * length, length)
            hi, lo = split(grid[pl.ds(start, length), :].T)
            his.append(jnp.concatenate([hi, turn(hi)], axis=1))
            los.append(jnp.concatenate([lo, turn(lo)], axis=1))
        pair = (jnp.concatenate(his, axis=0), jnp.concatenate(los, axis=0))
        other[whole, :] = row_product(pair, up)

    for z in range(planes):
        picks = [pl.ds(band * planes + z, 2 * length, stride=bz) for band in range(bands)]
        value = jnp.concatenate([other[pick, :] for pick in picks], axis=1)
        value = dot3((column_hi[...], column_lo[...]), split(value))
        weight = weights[pl.ds(z, length, stride=planes), :]
        weight = jnp.concatenate([weight] * 2, axis=0)
        weight = jnp.concatenate([weight] * bands, axis=1)
        value = dot3((back_hi[...], back_lo[...]), split(value * weight))
        for band, pick in enumerate(picks):
            grid[pick, :] = value[:, band * length : (band + 1) * length]

    @pl.loop(0, inner // batch)
    def _(step):
        his, los = [], []
        starts = [pl.multiple_of((step * batch + i) * length, length) for i in range(batch)]
        for start in starts:
            hi, lo = split(grid[pl.ds(start, length), :])
            his.append(jnp.concatenate([hi, turn(hi)], axis=1))
            los.append(jnp.concatenate([lo, turn(lo)], axis=1))
        pair = (jnp.concatenate(his, axis=0), jnp.concatenate(los, axis=0))
        value = row_product(pair, down)
        for i, start in enumerate(starts):
            out_ref[pl.ds(start, length), :] = value[i * length : (i + 1) * length].T


def depth_down(
    cols_ref,
    slot_ref,
    grid_ref,
    pw_ref,
    table_ref,
    out_ref,
    ready,
    field,
    sticks,
    flat,
    column,
    sent,
    got,
):
    peers = Peers()
    peers.greet()
    _, bands, rows, width = out_ref.shape
    devices, part_rows, _ = ready.shape
    planes = part_rows // 2
    own = 2 * rows
    length = devices * planes
    bz = bands * planes
    slots = LANES // (2 * bz)
    half = slots * bz
    group_rows = grid_ref.shape[0]
    shift = group_rows.bit_length() - 1
    group = math.gcd(own, GROUP)

    def gather(device):
        @pl.loop(0, own // group)
        def _(chunk):
            start = pl.multiple_of(chunk * group, group)
            first = device * own + start
            cols = [cols_ref[first + i] for i in range(group)]
            values = [grid_ref[pl.ds(col & (group_rows - 1), 1), :] for col in cols]
            for i, value in enumerate(values):
                sticks[pl.ds(start + i, 1), :] = value

        slot_of = lax.shift_right_logical(slot_ref[device], shift)

        tiles = []
        for tile in range(sticks.shape[0] // LANES):
            value = sticks[tile * LANES : (tile + 1) * LANES].T
            here = slot_of[:, tile * LANES : (tile + 1) * LANES]
            sums = []
            for part in range(2):
                total = value[part * half : part * half + bz]
                for slot in range(1, slots):
                    start = part * half + slot * bz
                    total = jnp.where(here == slot, value[start : start + bz], total)
                sums.append(total)
            tiles.append(jnp.concatenate(sums, axis=0))
        value = jnp.concatenate(tiles, axis=1)[:, :own]
        for part in range(2):
            for band in range(bands):
                start = (part * bands + band) * planes
                ready[
                    device, part * planes : (part + 1) * planes, band * own : (band + 1) * own
                ] = value[start : start + planes]

    sticks[...] = jnp.zeros_like(sticks)
    gather(peers.at(peers.step(1)))
    peers.met()
    peers.copy(peers.step(1), ready, field, sent, got).start()

    @pl.loop(2, devices)
    def _(turn):
        step = peers.step(turn)
        gather(peers.at(step))
        peers.copy(step, ready, field, sent, got).start()

    gather(peers.me)
    field[peers.me] = ready[peers.me]
    pw = pw_ref[...]
    first = lax.broadcasted_iota(jnp.int32, (rows, LANES), 1) < width // 2
    peers.settle(ready, field, sent, got)
    for device in range(devices):
        flat[device * part_rows : (device + 1) * part_rows] = field[device]
    value = dot3(split(flat[...]), (table_ref[0], table_ref[1]), ((0,), (0,)))
    column[0] = value[:, :length]
    column[1] = value[:, length:]
    for band in range(bands):
        for part in range(2):
            taken = []
            for parity in range(2):
                piece = column[part, pl.ds(band * own + parity, rows, stride=2), :]
                taken.append(
                    jnp.take_along_axis(piece, pw, axis=1, mode="promise_in_bounds")
                )
            out_ref[part, band] = jnp.where(first, taken[0], taken[1])


VM = pl.BlockSpec(memory_space=pltpu.VMEM)
SM = pl.BlockSpec(memory_space=pltpu.SMEM)
params = partial(pltpu.CompilerParams, vmem_limit_bytes=40 * 1024 * 1024)


def local(dpsi, stick_cols, pw_z, v_local, dv):
    devices = lax.axis_size("pencil") * lax.axis_size("tgroup")
    cores = lax.axis_size("tgroup")
    core = lax.axis_index("tgroup")
    length = math.isqrt(v_local.shape[1])
    planes = v_local.shape[0] // cores
    own = pw_z.shape[0] // cores
    zpw = pw_z.shape[1]
    bands = dpsi.shape[1]
    pairs = own // 2
    bz = bands * planes
    slots = LANES // (2 * bz)

    rows = lax.dynamic_slice_in_dim(pw_z, core * own, own, 0).reshape(pairs, 2 * zpw)
    coeff = (2, bands, pairs, 2 * zpw)
    by_wave = lax.dynamic_slice_in_dim(pw_z.T, core * own, own, 1)

    depth = jnp.asarray(np.stack(halves(depth_table(length, devices))))
    up, down = [jnp.asarray(np.concatenate(halves(table), axis=1)) for table in row_tables(length)]
    column = column_table(length, slots)
    back = [jnp.asarray(half) for half in halves(np.ascontiguousarray(column.T))]
    column = [jnp.asarray(half) for half in halves(column)]

    slot_cols = jnp.pad(stick_cols.reshape(devices, 1, own), ((0, 0), (0, 0), (0, -own % LANES)))
    block = (devices, 2 * planes, bands * own)
    in_slots = length // slots * length
    padded = -(-own // LANES) * LANES
    cost = pl.CostEstimate(
        flops=0, bytes_accessed=100 * math.prod(block) * 4, transcendentals=0
    )
    field = pl.pallas_call(
        depth_up,
        out_shape=jax.ShapeDtypeStruct(block, F32),
        in_specs=[VM] * 3,
        out_specs=VM,
        scratch_shapes=[
            pltpu.VMEM(block, F32),
            pltpu.VMEM(coeff, F32),
            pltpu.VMEM((padded, length), jnp.int32),
            pltpu.VMEM((2, bands * own, length), F32),
            pltpu.SemaphoreType.DMA((devices,)),
            pltpu.SemaphoreType.DMA((devices,)),
        ],
        cost_estimate=cost,
        compiler_params=params(collective_id=0, has_side_effects=True),
    )(dpsi, by_wave, depth)
    grid = pl.pallas_call(
        partial(plane_kernel, bands),
        out_shape=jax.ShapeDtypeStruct((in_slots, LANES), F32),
        in_specs=[SM] + [VM] * 9,
        out_specs=VM,
        scratch_shapes=[
            pltpu.VMEM((2 * bz, devices * own), F32),
            pltpu.VMEM((devices * own, LANES), F32),
            pltpu.VMEM((in_slots, LANES), F32),
            pltpu.VMEM((in_slots, LANES), F32),
            pltpu.VMEM((length * planes, length), F32),
        ],
        cost_estimate=cost,
        compiler_params=params(),
    )(stick_cols, field, v_local, dv, up, down, *column, *back)
    output = pl.pallas_call(
        depth_down,
        out_shape=jax.ShapeDtypeStruct(coeff, F32),
        in_specs=[SM] + [VM] * 4,
        out_specs=VM,
        scratch_shapes=[
            pltpu.VMEM(block, F32),
            pltpu.VMEM(block, F32),
            pltpu.VMEM((padded, LANES), F32),
            pltpu.VMEM((2 * length, bands * own), F32),
            pltpu.VMEM((2, bands * own, length), F32),
            pltpu.SemaphoreType.DMA((devices,)),
            pltpu.SemaphoreType.DMA((devices,)),
        ],
        cost_estimate=cost,
        compiler_params=params(collective_id=1, has_side_effects=True),
    )(stick_cols, slot_cols, grid, rows, depth)
    return output.reshape(dpsi.shape)


def solution(mesh):
    in_specs = (
        P(None, "pool", ("pencil", "tgroup")),
        P(),
        P("pencil", None),
        P("pencil", None),
        P("pencil", None),
    )
    out_specs = P(None, "pool", ("pencil", "tgroup"))
    return jax.shard_map(local, mesh=mesh, in_specs=in_specs, out_specs=out_specs, check_vma=False)
```

```python
from functools import partial
import math

import jax
import jax.numpy as jnp
import ml_dtypes
import numpy as np
from jax import lax
from jax.experimental import pallas as pl
from jax.experimental.pallas import tpu as pltpu
from jax.sharding import PartitionSpec as P

F32 = jnp.float32
BF16 = jnp.bfloat16
LANES = 128
GROUP = 32


def halves(table):
    hi = table.astype(ml_dtypes.bfloat16)
    lo = (table - hi.astype(np.float64)).astype(ml_dtypes.bfloat16)
    return hi, lo


def split(value):
    hi = value.astype(BF16)
    lo = (value - hi.astype(F32)).astype(BF16)
    return hi, lo


def dot3(left, right, dims=((1,), (0,))):
    mul = lambda a, b: lax.dot_general(a, b, (dims, ((), ())), preferred_element_type=F32)
    return mul(left[0], right[0]) + (mul(left[0], right[1]) + mul(left[1], right[0]))


def waves(length):
    k = np.arange(length)
    angle = (k[:, None] * k[None, :] % length) * (2.0 * math.pi / length)
    return np.cos(angle) / math.sqrt(length), np.sin(angle) / math.sqrt(length)


def depth_table(length, devices):
    cos, sin = waves(length)
    planes = length // devices
    whole = np.stack([np.stack([cos, -sin], 1), np.stack([sin, cos], 1)])
    whole = whole.reshape(2, devices, planes, 2 * length)
    return whole.transpose(1, 0, 2, 3).reshape(2 * length, 2 * length)


def row_tables(length):
    cos, sin = waves(length)
    return np.concatenate([cos, sin]), np.concatenate([cos, -sin])


def column_table(length, slots):
    cos, sin = waves(length)
    whole = np.stack([np.stack([cos, -sin], 1), np.stack([sin, cos], 1)])
    whole = whole.reshape(2, length, 2, slots, length // slots)
    return whole.transpose(0, 1, 4, 2, 3).reshape(2 * length, 2 * length)


class Peers:
    def __init__(self):
        self.cores = lax.axis_size("tgroup")
        self.count = lax.axis_size("pencil") * self.cores
        self.me = lax.axis_index("pencil") * self.cores + lax.axis_index("tgroup")
        self.barrier = pltpu.get_barrier_semaphore()

    def at(self, step):
        return lax.rem(self.me + step, self.count)

    def step(self, turn):
        away = lax.div(turn, 2)
        return self.count // 2 + jnp.where(lax.rem(turn, 2) == 0, away, -away)

    def name(self, device):
        return {"pencil": lax.div(device, self.cores), "tgroup": lax.rem(device, self.cores)}

    def greet(self):
        @pl.loop(1, self.count)
        def _(step):
            pl.semaphore_signal(
                self.barrier,
                inc=1,
                device_id=self.name(self.at(step)),
                device_id_type=pl.DeviceIdType.MESH,
            )

    def met(self):
        pl.semaphore_wait(self.barrier, self.count - 1)

    def copy(self, step, source, target, sent, got):
        peer = self.at(step)
        return pltpu.make_async_remote_copy(
            src_ref=source.at[peer],
            dst_ref=target.at[self.me],
            send_sem=sent.at[step],
            recv_sem=got.at[step],
            device_id=self.name(peer),
            device_id_type=pl.DeviceIdType.MESH,
        )

    def settle(self, source, target, sent, got):
        @pl.loop(1, self.count)
        def _(step):
            self.copy(step, source, target, sent, got).wait()


def depth_up(
    coeff_ref,
    pw_ref,
    table_ref,
    out_ref,
    ready,
    coeff,
    inverse,
    column,
    sent,
    got,
):
    peers = Peers()
    peers.greet()
    bands = coeff_ref.shape[1]
    _, _, rows, width = coeff.shape
    devices, part_rows, _ = out_ref.shape
    zpw, own = pw_ref.shape
    length = inverse.shape[1]
    for part in range(2):
        for band in range(bands):
            for row in range(rows):
                coeff[part, band, row : row + 1] = coeff_ref[
                    part, band : band + 1, row * width : (row + 1) * width
                ]
    z = lax.broadcasted_iota(jnp.int32, (length, LANES), 0)
    for tile in range(own // LANES + (own % LANES > 0)):
        lanes = slice(tile * LANES, min((tile + 1) * LANES, own))
        source = jnp.full((length, LANES), -1, jnp.int32)
        for k in range(zpw):
            row = pw_ref[k : k + 1, lanes]
            if row.shape[1] < LANES:
                row = jnp.concatenate(
                    [row, jnp.full((1, LANES - row.shape[1]), -1, jnp.int32)], axis=1
                )
            source = jnp.where(row == z, k, source)
        inverse[tile * LANES : (tile + 1) * LANES] = source.T
    for parity in range(2):
        source = inverse[pl.ds(parity, rows, stride=2), :]
        found = source >= 0
        source = jnp.maximum(source, 0) + parity * zpw
        for band in range(bands):
            places = pl.ds(band * own + parity, rows, stride=2)
            for part in range(2):
                taken = jnp.take_along_axis(
                    coeff[part, band], source, axis=1, mode="promise_in_bounds"
                )
                column[part, places, :] = jnp.where(found, taken, 0.0)
    value = jnp.concatenate([column[0], column[1]], axis=1)
    field = dot3((table_ref[0], table_ref[1]), split(value), ((1,), (1,)))
    for device in range(devices):
        ready[device] = field[device * part_rows : (device + 1) * part_rows]
    peers.met()

    @pl.loop(1, devices)
    def _(turn):
        peers.copy(peers.step(turn), ready, out_ref, sent, got).start()

    out_ref[peers.me] = ready[peers.me]
    peers.settle(ready, out_ref, sent, got)


def turn(value):
    half = value.shape[0] // 2
    return jnp.concatenate([-value[half:], value[:half]], axis=0)


def row_product(pair, table):
    length = table.shape[1] // 2
    mul = partial(jnp.dot, preferred_element_type=F32)
    both = mul(pair[0], table[...])
    return both[:, :length] + (both[:, length:] + mul(pair[1], table[:, :length]))


def plane_kernel(
    bands,
    cols_ref,
    field_ref,
    weight_ref,
    table_ref,
    out_ref,
    flat,
    sticks,
    grid,
    other,
):
    devices, part_rows, block = field_ref.shape
    planes = part_rows // 2
    own = block // bands
    length = weight_ref.shape[1]
    bz = bands * planes
    slots = LANES // (2 * bz)
    inner = length // slots
    group_rows = inner * length
    batch = math.gcd(inner, 8)
    total = devices * own
    shift = group_rows.bit_length() - 1

    grid[...] = jnp.zeros_like(grid)
    for device in range(devices):
        for part in range(2):
            for band in range(bands):
                flat[
                    (part * bands + band) * planes : (part * bands + band + 1) * planes,
                    device * own : (device + 1) * own,
                ] = field_ref[
                    device, part * planes : (part + 1) * planes, band * own : (band + 1) * own
                ]
    for tile in range(total // LANES):
        value = flat[:, tile * LANES : (tile + 1) * LANES]
        value = jnp.concatenate([value[:bz]] * slots + [value[bz:]] * slots, axis=0)
        sticks[tile * LANES : (tile + 1) * LANES] = value.T

    lane = lax.broadcasted_iota(jnp.int32, (1, LANES), 1)
    slot_of_lane = lane // bz % slots

    @pl.loop(0, total // GROUP)
    def _(step):
        base = pl.multiple_of(step * GROUP, GROUP)
        cols = [cols_ref[base + i] for i in range(GROUP)]
        rows = [col & (group_rows - 1) for col in cols]
        masks = [slot_of_lane == lax.shift_right_logical(col, shift) for col in cols]
        values = [sticks[pl.ds(base + i, 1), :] for i in range(GROUP)]
        for value, row, mask in zip(values, rows, masks):
            pltpu.store(grid.at[pl.ds(row, 1), :], value, mask=mask)

    @pl.loop(0, inner // batch)
    def _(step):
        whole = pl.ds(pl.multiple_of(step * batch * length, batch * length), batch * length)
        his, los = [], []
        for i in range(batch):
            start = pl.multiple_of((step * batch + i) * length, length)
            hi, lo = split(grid[pl.ds(start, length), :].T)
            his.append(jnp.concatenate([hi, turn(hi)], axis=1))
            los.append(jnp.concatenate([lo, turn(lo)], axis=1))
        pair = (jnp.concatenate(his, axis=0), jnp.concatenate(los, axis=0))
        other[whole, :] = row_product(pair, table_ref[2])

    for z in range(planes):
        picks = [pl.ds(band * planes + z, 2 * length, stride=bz) for band in range(bands)]
        value = jnp.concatenate([other[pick, :] for pick in picks], axis=1)
        value = dot3((table_ref[4], table_ref[5]), split(value))
        weight = weight_ref[pl.ds(z, length, stride=planes), :]
        weight = jnp.concatenate([weight] * 2, axis=0)
        weight = jnp.concatenate([weight] * bands, axis=1)
        value = dot3((table_ref[6], table_ref[7]), split(value * weight))
        for band, pick in enumerate(picks):
            grid[pick, :] = value[:, band * length : (band + 1) * length]

    @pl.loop(0, inner // batch)
    def _(step):
        his, los = [], []
        starts = [pl.multiple_of((step * batch + i) * length, length) for i in range(batch)]
        for start in starts:
            hi, lo = split(grid[pl.ds(start, length), :])
            his.append(jnp.concatenate([hi, turn(hi)], axis=1))
            los.append(jnp.concatenate([lo, turn(lo)], axis=1))
        pair = (jnp.concatenate(his, axis=0), jnp.concatenate(los, axis=0))
        value = row_product(pair, table_ref[3])
        for i, start in enumerate(starts):
            out_ref[pl.ds(start, length), :] = value[i * length : (i + 1) * length].T


def depth_down(
    cols_ref,
    slot_ref,
    grid_ref,
    pw_ref,
    table_ref,
    out_ref,
    ready,
    field,
    sticks,
    flat,
    column,
    sent,
    got,
):
    peers = Peers()
    peers.greet()
    _, bands, rows, width = out_ref.shape
    devices, part_rows, _ = ready.shape
    planes = part_rows // 2
    own = 2 * rows
    length = devices * planes
    bz = bands * planes
    slots = LANES // (2 * bz)
    half = slots * bz
    group_rows = grid_ref.shape[0]
    shift = group_rows.bit_length() - 1
    group = math.gcd(own, GROUP)

    def gather(device):
        @pl.loop(0, own // group)
        def _(chunk):
            start = pl.multiple_of(chunk * group, group)
            first = device * own + start
            cols = [cols_ref[first + i] for i in range(group)]
            values = [grid_ref[pl.ds(col & (group_rows - 1), 1), :] for col in cols]
            for i, value in enumerate(values):
                sticks[pl.ds(start + i, 1), :] = value

        slot_of = lax.shift_right_logical(slot_ref[device], shift)

        tiles = []
        for tile in range(sticks.shape[0] // LANES):
            value = sticks[tile * LANES : (tile + 1) * LANES].T
            here = slot_of[:, tile * LANES : (tile + 1) * LANES]
            sums = []
            for part in range(2):
                total = value[part * half : part * half + bz]
                for slot in range(1, slots):
                    start = part * half + slot * bz
                    total = jnp.where(here == slot, value[start : start + bz], total)
                sums.append(total)
            tiles.append(jnp.concatenate(sums, axis=0))
        value = jnp.concatenate(tiles, axis=1)[:, :own]
        for part in range(2):
            for band in range(bands):
                start = (part * bands + band) * planes
                ready[
                    device, part * planes : (part + 1) * planes, band * own : (band + 1) * own
                ] = value[start : start + planes]

    sticks[...] = jnp.zeros_like(sticks)
    gather(peers.at(peers.step(1)))
    peers.met()
    peers.copy(peers.step(1), ready, field, sent, got).start()

    @pl.loop(2, devices)
    def _(turn):
        step = peers.step(turn)
        gather(peers.at(step))
        peers.copy(step, ready, field, sent, got).start()

    gather(peers.me)
    field[peers.me] = ready[peers.me]
    pw = pw_ref[...]
    first = lax.broadcasted_iota(jnp.int32, (rows, LANES), 1) < width // 2
    peers.settle(ready, field, sent, got)
    for device in range(devices):
        flat[device * part_rows : (device + 1) * part_rows] = field[device]
    value = dot3(split(flat[...]), (table_ref[0], table_ref[1]), ((0,), (0,)))
    column[0] = value[:, :length]
    column[1] = value[:, length:]
    for band in range(bands):
        for part in range(2):
            taken = []
            for parity in range(2):
                piece = column[part, pl.ds(band * own + parity, rows, stride=2), :]
                taken.append(
                    jnp.take_along_axis(piece, pw, axis=1, mode="promise_in_bounds")
                )
            out_ref[part, band] = jnp.where(first, taken[0], taken[1])


VM = pl.BlockSpec(memory_space=pltpu.VMEM)
SM = pl.BlockSpec(memory_space=pltpu.SMEM)
params = partial(pltpu.CompilerParams, vmem_limit_bytes=40 * 1024 * 1024)


def local(dpsi, stick_cols, pw_z, v_local, dv):
    devices = lax.axis_size("pencil") * lax.axis_size("tgroup")
    cores = lax.axis_size("tgroup")
    core = lax.axis_index("tgroup")
    length = math.isqrt(v_local.shape[1])
    planes = v_local.shape[0] // cores
    own = pw_z.shape[0] // cores
    zpw = pw_z.shape[1]
    bands = dpsi.shape[1]
    pairs = own // 2
    bz = bands * planes
    slots = LANES // (2 * bz)

    rows = lax.dynamic_slice_in_dim(pw_z, core * own, own, 0).reshape(pairs, 2 * zpw)
    coeff = (2, bands, pairs, 2 * zpw)
    by_wave = lax.dynamic_slice_in_dim(pw_z.T, core * own, own, 1)

    column = column_table(length, slots)
    tables = list(halves(depth_table(length, devices)))
    tables += [np.concatenate(halves(table), axis=1) for table in row_tables(length)]
    tables += halves(column) + halves(np.ascontiguousarray(column.T))
    tables = jnp.asarray(np.stack(tables))
    potential = lax.dynamic_slice_in_dim(v_local, core * planes, planes, 0)
    potential = potential + lax.dynamic_slice_in_dim(dv, core * planes, planes, 0)
    potential = potential.reshape(planes, length, length).transpose(1, 0, 2)
    by_wave, potential = lax.optimization_barrier((by_wave, potential))
    potential = potential.reshape(length * planes, length)

    slot_cols = jnp.pad(stick_cols.reshape(devices, 1, own), ((0, 0), (0, 0), (0, -own % LANES)))
    block = (devices, 2 * planes, bands * own)
    in_slots = length // slots * length
    padded = -(-own // LANES) * LANES
    cost = pl.CostEstimate(
        flops=0, bytes_accessed=100 * math.prod(block) * 4, transcendentals=0
    )
    field = pl.pallas_call(
        depth_up,
        out_shape=jax.ShapeDtypeStruct(block, F32),
        in_specs=[VM] * 3,
        out_specs=VM,
        scratch_shapes=[
            pltpu.VMEM(block, F32),
            pltpu.VMEM(coeff, F32),
            pltpu.VMEM((padded, length), jnp.int32),
            pltpu.VMEM((2, bands * own, length), F32),
            pltpu.SemaphoreType.DMA((devices,)),
            pltpu.SemaphoreType.DMA((devices,)),
        ],
        cost_estimate=cost,
        compiler_params=params(collective_id=0, has_side_effects=True),
    )(dpsi, by_wave, tables)
    grid = pl.pallas_call(
        partial(plane_kernel, bands),
        out_shape=jax.ShapeDtypeStruct((in_slots, LANES), F32),
        in_specs=[SM] + [VM] * 3,
        out_specs=VM,
        scratch_shapes=[
            pltpu.VMEM((2 * bz, devices * own), F32),
            pltpu.VMEM((devices * own, LANES), F32),
            pltpu.VMEM((in_slots, LANES), F32),
            pltpu.VMEM((in_slots, LANES), F32),
        ],
        cost_estimate=cost,
        compiler_params=params(),
    )(stick_cols, field, potential, tables)
    output = pl.pallas_call(
        depth_down,
        out_shape=jax.ShapeDtypeStruct(coeff, F32),
        in_specs=[SM] + [VM] * 4,
        out_specs=VM,
        scratch_shapes=[
            pltpu.VMEM(block, F32),
            pltpu.VMEM(block, F32),
            pltpu.VMEM((padded, LANES), F32),
            pltpu.VMEM((2 * length, bands * own), F32),
            pltpu.VMEM((2, bands * own, length), F32),
            pltpu.SemaphoreType.DMA((devices,)),
            pltpu.SemaphoreType.DMA((devices,)),
        ],
        cost_estimate=cost,
        compiler_params=params(collective_id=1, has_side_effects=True),
    )(stick_cols, slot_cols, grid, rows, tables)
    return output.reshape(dpsi.shape)


def solution(mesh):
    in_specs = (
        P(None, "pool", ("pencil", "tgroup")),
        P(),
        P("pencil", None),
        P("pencil", None),
        P("pencil", None),
    )
    out_specs = P(None, "pool", ("pencil", "tgroup"))
    return jax.shard_map(local, mesh=mesh, in_specs=in_specs, out_specs=out_specs, check_vma=False)
```

```python
from functools import partial
import math

import jax
import jax.numpy as jnp
import ml_dtypes
import numpy as np
from jax import lax
from jax.experimental import pallas as pl
from jax.experimental.pallas import tpu as pltpu
from jax.sharding import PartitionSpec as P

F32 = jnp.float32
BF16 = jnp.bfloat16
LANES = 128
GROUP = 32


def halves(table):
    hi = table.astype(ml_dtypes.bfloat16)
    lo = (table - hi.astype(np.float64)).astype(ml_dtypes.bfloat16)
    return hi, lo


def split(value):
    hi = value.astype(BF16)
    lo = (value - hi.astype(F32)).astype(BF16)
    return hi, lo


def dot3(left, right, dims=((1,), (0,))):
    mul = lambda a, b: lax.dot_general(a, b, (dims, ((), ())), preferred_element_type=F32)
    return mul(left[0], right[0]) + (mul(left[0], right[1]) + mul(left[1], right[0]))


def waves(length):
    k = np.arange(length)
    angle = (k[:, None] * k[None, :] % length) * (2.0 * math.pi / length)
    return np.cos(angle) / math.sqrt(length), np.sin(angle) / math.sqrt(length)


def depth_table(length, devices):
    cos, sin = waves(length)
    planes = length // devices
    whole = np.stack([np.stack([cos, -sin], 1), np.stack([sin, cos], 1)])
    whole = whole.reshape(2, devices, planes, 2 * length)
    return whole.transpose(1, 0, 2, 3).reshape(2 * length, 2 * length)


def row_tables(length):
    cos, sin = waves(length)
    return np.concatenate([cos, sin]), np.concatenate([cos, -sin])


def column_table(length, slots):
    cos, sin = waves(length)
    whole = np.stack([np.stack([cos, -sin], 1), np.stack([sin, cos], 1)])
    whole = whole.reshape(2, length, 2, slots, length // slots)
    return whole.transpose(0, 1, 4, 2, 3).reshape(2 * length, 2 * length)


class Peers:
    def __init__(self):
        self.cores = lax.axis_size("tgroup")
        self.count = lax.axis_size("pencil") * self.cores
        self.me = lax.axis_index("pencil") * self.cores + lax.axis_index("tgroup")
        self.barrier = pltpu.get_barrier_semaphore()

    def at(self, step):
        return lax.rem(self.me + step, self.count)

    def step(self, turn):
        away = lax.div(turn, 2)
        return self.count // 2 + jnp.where(lax.rem(turn, 2) == 0, away, -away)

    def name(self, device):
        return {"pencil": lax.div(device, self.cores), "tgroup": lax.rem(device, self.cores)}

    def greet(self):
        @pl.loop(1, self.count)
        def _(step):
            pl.semaphore_signal(
                self.barrier,
                inc=1,
                device_id=self.name(self.at(step)),
                device_id_type=pl.DeviceIdType.MESH,
            )

    def met(self):
        pl.semaphore_wait(self.barrier, self.count - 1)

    def copy(self, step, source, target, sent, got):
        peer = self.at(step)
        return pltpu.make_async_remote_copy(
            src_ref=source.at[peer],
            dst_ref=target.at[self.me],
            send_sem=sent.at[step],
            recv_sem=got.at[step],
            device_id=self.name(peer),
            device_id_type=pl.DeviceIdType.MESH,
        )

    def settle(self, source, target, sent, got):
        @pl.loop(1, self.count)
        def _(step):
            self.copy(step, source, target, sent, got).wait()


def depth_up(
    coeff_ref,
    pw_ref,
    table_ref,
    out_ref,
    ready,
    coeff,
    inverse,
    column,
    sent,
    got,
):
    peers = Peers()
    peers.greet()
    bands = coeff_ref.shape[1]
    _, _, rows, width = coeff.shape
    devices, part_rows, _ = out_ref.shape
    zpw, own = pw_ref.shape
    length = inverse.shape[1]
    for part in range(2):
        for band in range(bands):
            for start in range(0, rows, 3 * GROUP // 2):
                some = range(start, min(start + 3 * GROUP // 2, rows))
                values = [
                    coeff_ref[part, band : band + 1, row * width : (row + 1) * width]
                    for row in some
                ]
                for row, value in zip(some, values):
                    coeff[part, band, row : row + 1] = value
    z = lax.broadcasted_iota(jnp.int32, (length, LANES), 0)
    for tile in range(own // LANES + (own % LANES > 0)):
        lanes = slice(tile * LANES, min((tile + 1) * LANES, own))
        source = jnp.full((length, LANES), -1, jnp.int32)
        for k in range(zpw):
            row = pw_ref[k : k + 1, lanes]
            if row.shape[1] < LANES:
                row = jnp.concatenate(
                    [row, jnp.full((1, LANES - row.shape[1]), -1, jnp.int32)], axis=1
                )
            source = jnp.where(row == z, k, source)
        inverse[tile * LANES : (tile + 1) * LANES] = source.T
    for parity in range(2):
        source = inverse[pl.ds(parity, rows, stride=2), :]
        found = source >= 0
        source = jnp.maximum(source, 0) + parity * zpw
        for band in range(bands):
            places = pl.ds(band * own + parity, rows, stride=2)
            for part in range(2):
                taken = jnp.take_along_axis(
                    coeff[part, band], source, axis=1, mode="promise_in_bounds"
                )
                column[part, places, :] = jnp.where(found, taken, 0.0)
    value = jnp.concatenate([column[0], column[1]], axis=1)
    field = dot3((table_ref[0], table_ref[1]), split(value), ((1,), (1,)))
    for device in range(devices):
        ready[device] = field[device * part_rows : (device + 1) * part_rows]
    peers.met()

    @pl.loop(1, devices)
    def _(turn):
        peers.copy(peers.step(turn), ready, out_ref, sent, got).start()

    out_ref[peers.me] = ready[peers.me]
    peers.settle(ready, out_ref, sent, got)


def turn(value):
    half = value.shape[0] // 2
    return jnp.concatenate([-value[half:], value[:half]], axis=0)


def row_product(pair, table):
    length = table.shape[1] // 2
    mul = partial(jnp.dot, preferred_element_type=F32)
    both = mul(pair[0], table[...])
    return both[:, :length] + (both[:, length:] + mul(pair[1], table[:, :length]))


def plane_kernel(
    bands,
    cols_ref,
    field_ref,
    weight_ref,
    table_ref,
    out_ref,
    flat,
    sticks,
    grid,
    other,
):
    devices, part_rows, block = field_ref.shape
    planes = part_rows // 2
    own = block // bands
    length = weight_ref.shape[1]
    bz = bands * planes
    slots = LANES // (2 * bz)
    inner = length // slots
    group_rows = inner * length
    batch = math.gcd(inner, 8)
    total = devices * own

    grid[...] = jnp.zeros_like(grid)
    for part in range(2):
        for band in range(bands):
            start = (part * bands + band) * planes
            values = [
                field_ref[
                    device, part * planes : (part + 1) * planes, band * own : (band + 1) * own
                ]
                for device in range(devices)
            ]
            for device, value in enumerate(values):
                flat[start : start + planes, device * own : (device + 1) * own] = value
    for start in range(0, total // LANES, 6):
        some = range(start, min(start + 6, total // LANES))
        values = [flat[:, tile * LANES : (tile + 1) * LANES] for tile in some]
        for tile, value in zip(some, values):
            value = jnp.concatenate([value[:bz]] * slots + [value[bz:]] * slots, axis=0)
            sticks[tile * LANES : (tile + 1) * LANES] = value.T

    lane = lax.broadcasted_iota(jnp.int32, (1, LANES), 1)
    first_of_lane = (lane // bz % slots) * group_rows
    group = GROUP // 2

    def fetch(step):
        base = pl.multiple_of(step * group, group)
        cols = [cols_ref[base + i] for i in range(group)]
        return cols, [sticks[pl.ds(base + i, 1), :] for i in range(group)]

    def scatter(cols, values):
        for col, value in zip(cols, values):
            spread = jnp.full((1, LANES), col, jnp.int32)
            mask = (spread & -group_rows) == first_of_lane
            pltpu.store(grid.at[pl.ds(col & (group_rows - 1), 1), :], value, mask=mask)

    def each(step, held):
        following = fetch(step)
        scatter(*held)
        return following

    scatter(*lax.fori_loop(1, total // group, each, fetch(0)))

    @pl.loop(0, inner // batch)
    def _(step):
        whole = pl.ds(pl.multiple_of(step * batch * length, batch * length), batch * length)
        his, los = [], []
        for i in range(batch):
            start = pl.multiple_of((step * batch + i) * length, length)
            hi, lo = split(grid[pl.ds(start, length), :].T)
            his.append(jnp.concatenate([hi, turn(hi)], axis=1))
            los.append(jnp.concatenate([lo, turn(lo)], axis=1))
        pair = (jnp.concatenate(his, axis=0), jnp.concatenate(los, axis=0))
        other[whole, :] = row_product(pair, table_ref[2])

    def picks(z):
        return [pl.ds(band * planes + z, 2 * length, stride=bz) for band in range(bands)]

    def planes_of(z):
        return split(jnp.concatenate([other[pick, :] for pick in picks(z)], axis=1))

    following = planes_of(0)
    for z in range(planes):
        value = dot3((table_ref[4], table_ref[5]), following)
        if z + 1 < planes:
            following = planes_of(z + 1)
        weight = weight_ref[pl.ds(z, length, stride=planes), :]
        weight = jnp.concatenate([weight] * 2, axis=0)
        weight = jnp.concatenate([weight] * bands, axis=1)
        value = dot3((table_ref[6], table_ref[7]), split(value * weight))
        for band, pick in enumerate(picks(z)):
            grid[pick, :] = value[:, band * length : (band + 1) * length]

    @pl.loop(0, inner // batch)
    def _(step):
        his, los = [], []
        starts = [pl.multiple_of((step * batch + i) * length, length) for i in range(batch)]
        for start in starts:
            hi, lo = split(grid[pl.ds(start, length), :])
            his.append(jnp.concatenate([hi, turn(hi)], axis=1))
            los.append(jnp.concatenate([lo, turn(lo)], axis=1))
        pair = (jnp.concatenate(his, axis=0), jnp.concatenate(los, axis=0))
        value = row_product(pair, table_ref[3])
        for i, start in enumerate(starts):
            out_ref[pl.ds(start, length), :] = value[i * length : (i + 1) * length].T


def depth_down(
    cols_ref,
    slot_ref,
    grid_ref,
    pw_ref,
    table_ref,
    out_ref,
    ready,
    field,
    sticks,
    flat,
    column,
    sent,
    got,
):
    peers = Peers()
    peers.greet()
    _, bands, rows, width = out_ref.shape
    devices, part_rows, _ = ready.shape
    planes = part_rows // 2
    own = 2 * rows
    length = devices * planes
    bz = bands * planes
    slots = LANES // (2 * bz)
    half = slots * bz
    group_rows = grid_ref.shape[0]
    shift = group_rows.bit_length() - 1
    group = math.gcd(own, GROUP // 2)

    def gather(device):
        def fetch(chunk):
            first = device * own + chunk * group
            cols = [cols_ref[first + i] for i in range(group)]
            return [grid_ref[pl.ds(col & (group_rows - 1), 1), :] for col in cols]

        def put(chunk, values):
            start = pl.multiple_of(chunk * group, group)
            for i, value in enumerate(values):
                sticks[pl.ds(start + i, 1), :] = value

        def each(chunk, held):
            following = fetch(chunk)
            put(chunk - 1, held)
            return following

        chunks = own // group
        put(chunks - 1, lax.fori_loop(1, chunks, each, fetch(0)))

        slot_of = lax.shift_right_logical(slot_ref[device], shift)

        tiles = []
        for tile in range(sticks.shape[0] // LANES):
            value = sticks[tile * LANES : (tile + 1) * LANES].T
            here = slot_of[:, tile * LANES : (tile + 1) * LANES]
            sums = []
            for part in range(2):
                total = value[part * half : part * half + bz]
                for slot in range(1, slots):
                    start = part * half + slot * bz
                    total = jnp.where(here == slot, value[start : start + bz], total)
                sums.append(total)
            tiles.append(jnp.concatenate(sums, axis=0))
        value = jnp.concatenate(tiles, axis=1)[:, :own]
        for part in range(2):
            for band in range(bands):
                start = (part * bands + band) * planes
                ready[
                    device, part * planes : (part + 1) * planes, band * own : (band + 1) * own
                ] = value[start : start + planes]

    sticks[...] = jnp.zeros_like(sticks)
    gather(peers.at(peers.step(1)))
    peers.met()
    peers.copy(peers.step(1), ready, field, sent, got).start()

    @pl.loop(2, devices)
    def _(turn):
        step = peers.step(turn)
        gather(peers.at(step))
        peers.copy(step, ready, field, sent, got).start()

    gather(peers.me)
    field[peers.me] = ready[peers.me]
    pw = pw_ref[...]
    first = lax.broadcasted_iota(jnp.int32, (rows, LANES), 1) < width // 2
    peers.settle(ready, field, sent, got)
    for device in range(devices):
        flat[device * part_rows : (device + 1) * part_rows] = field[device]
    value = dot3(split(flat[...]), (table_ref[0], table_ref[1]), ((0,), (0,)))
    column[0] = value[:, :length]
    column[1] = value[:, length:]
    for band in range(bands):
        for part in range(2):
            taken = []
            for parity in range(2):
                piece = column[part, pl.ds(band * own + parity, rows, stride=2), :]
                taken.append(
                    jnp.take_along_axis(piece, pw, axis=1, mode="promise_in_bounds")
                )
            out_ref[part, band] = jnp.where(first, taken[0], taken[1])


VM = pl.BlockSpec(memory_space=pltpu.VMEM)
SM = pl.BlockSpec(memory_space=pltpu.SMEM)
params = partial(pltpu.CompilerParams, vmem_limit_bytes=40 * 1024 * 1024)


def local(dpsi, stick_cols, pw_z, v_local, dv):
    devices = lax.axis_size("pencil") * lax.axis_size("tgroup")
    cores = lax.axis_size("tgroup")
    core = lax.axis_index("tgroup")
    length = math.isqrt(v_local.shape[1])
    planes = v_local.shape[0] // cores
    own = pw_z.shape[0] // cores
    zpw = pw_z.shape[1]
    bands = dpsi.shape[1]
    pairs = own // 2
    bz = bands * planes
    slots = LANES // (2 * bz)

    rows = lax.dynamic_slice_in_dim(pw_z, core * own, own, 0).reshape(pairs, 2 * zpw)
    coeff = (2, bands, pairs, 2 * zpw)
    by_wave = lax.dynamic_slice_in_dim(pw_z.T, core * own, own, 1)

    column = column_table(length, slots)
    tables = list(halves(depth_table(length, devices)))
    tables += [np.concatenate(halves(table), axis=1) for table in row_tables(length)]
    tables += halves(column) + halves(np.ascontiguousarray(column.T))
    tables = jnp.asarray(np.stack(tables))
    potential = lax.dynamic_slice_in_dim(v_local, core * planes, planes, 0)
    potential = potential + lax.dynamic_slice_in_dim(dv, core * planes, planes, 0)
    potential = potential.reshape(planes, length, length).transpose(1, 0, 2)
    by_wave, potential = lax.optimization_barrier((by_wave, potential))
    potential = potential.reshape(length * planes, length)

    slot_cols = jnp.pad(stick_cols.reshape(devices, 1, own), ((0, 0), (0, 0), (0, -own % LANES)))
    block = (devices, 2 * planes, bands * own)
    in_slots = length // slots * length
    padded = -(-own // LANES) * LANES
    cost = pl.CostEstimate(
        flops=0, bytes_accessed=100 * math.prod(block) * 4, transcendentals=0
    )
    field = pl.pallas_call(
        depth_up,
        out_shape=jax.ShapeDtypeStruct(block, F32),
        in_specs=[VM] * 3,
        out_specs=VM,
        scratch_shapes=[
            pltpu.VMEM(block, F32),
            pltpu.VMEM(coeff, F32),
            pltpu.VMEM((padded, length), jnp.int32),
            pltpu.VMEM((2, bands * own, length), F32),
            pltpu.SemaphoreType.DMA((devices,)),
            pltpu.SemaphoreType.DMA((devices,)),
        ],
        cost_estimate=cost,
        compiler_params=params(collective_id=0, has_side_effects=True),
    )(dpsi, by_wave, tables)
    grid = pl.pallas_call(
        partial(plane_kernel, bands),
        out_shape=jax.ShapeDtypeStruct((in_slots, LANES), F32),
        in_specs=[SM] + [VM] * 3,
        out_specs=VM,
        scratch_shapes=[
            pltpu.VMEM((2 * bz, devices * own), F32),
            pltpu.VMEM((devices * own, LANES), F32),
            pltpu.VMEM((in_slots, LANES), F32),
            pltpu.VMEM((in_slots, LANES), F32),
        ],
        cost_estimate=cost,
        compiler_params=params(),
    )(stick_cols, field, potential, tables)
    output = pl.pallas_call(
        depth_down,
        out_shape=jax.ShapeDtypeStruct(coeff, F32),
        in_specs=[SM] + [VM] * 4,
        out_specs=VM,
        scratch_shapes=[
            pltpu.VMEM(block, F32),
            pltpu.VMEM(block, F32),
            pltpu.VMEM((padded, LANES), F32),
            pltpu.VMEM((2 * length, bands * own), F32),
            pltpu.VMEM((2, bands * own, length), F32),
            pltpu.SemaphoreType.DMA((devices,)),
            pltpu.SemaphoreType.DMA((devices,)),
        ],
        cost_estimate=cost,
        compiler_params=params(collective_id=1, has_side_effects=True),
    )(stick_cols, slot_cols, grid, rows, tables)
    return output.reshape(dpsi.shape)


def solution(mesh):
    in_specs = (
        P(None, "pool", ("pencil", "tgroup")),
        P(),
        P("pencil", None),
        P("pencil", None),
        P("pencil", None),
    )
    out_specs = P(None, "pool", ("pencil", "tgroup"))
    return jax.shard_map(local, mesh=mesh, in_specs=in_specs, out_specs=out_specs, check_vma=False)
```

```python
from functools import partial
import math

import jax
import jax.numpy as jnp
import ml_dtypes
import numpy as np
from jax import lax
from jax.experimental import pallas as pl
from jax.experimental.pallas import tpu as pltpu
from jax.sharding import PartitionSpec as P

F32 = jnp.float32
BF16 = jnp.bfloat16
LANES = 128
GROUP = 32


def halves(table):
    hi = table.astype(ml_dtypes.bfloat16)
    lo = (table - hi.astype(np.float64)).astype(ml_dtypes.bfloat16)
    return hi, lo


def split(value):
    hi = value.astype(BF16)
    lo = (value - hi.astype(F32)).astype(BF16)
    return hi, lo


def dot3(left, right, dims=((1,), (0,))):
    mul = lambda a, b: lax.dot_general(a, b, (dims, ((), ())), preferred_element_type=F32)
    return mul(left[0], right[0]) + (mul(left[0], right[1]) + mul(left[1], right[0]))


def waves(length):
    k = np.arange(length)
    angle = (k[:, None] * k[None, :] % length) * (2.0 * math.pi / length)
    return np.cos(angle) / math.sqrt(length), np.sin(angle) / math.sqrt(length)


def depth_table(length, devices):
    cos, sin = waves(length)
    planes = length // devices
    whole = np.stack([np.stack([cos, -sin], 1), np.stack([sin, cos], 1)])
    whole = whole.reshape(2, devices, planes, 2 * length)
    return whole.transpose(1, 0, 2, 3).reshape(2 * length, 2 * length)


def row_tables(length):
    cos, sin = waves(length)
    return np.concatenate([cos, sin]), np.concatenate([cos, -sin])


def column_table(length, slots):
    cos, sin = waves(length)
    whole = np.stack([np.stack([cos, -sin], 1), np.stack([sin, cos], 1)])
    whole = whole.reshape(2, length, 2, slots, length // slots)
    return whole.transpose(0, 1, 4, 2, 3).reshape(2 * length, 2 * length)


class Peers:
    def __init__(self):
        self.cores = lax.axis_size("tgroup")
        self.count = lax.axis_size("pencil") * self.cores
        self.me = lax.axis_index("pencil") * self.cores + lax.axis_index("tgroup")
        self.barrier = pltpu.get_barrier_semaphore()

    def at(self, step):
        return lax.rem(self.me + step, self.count)

    def step(self, turn):
        away = lax.div(turn, 2)
        return self.count // 2 + jnp.where(lax.rem(turn, 2) == 0, away, -away)

    def name(self, device):
        return {"pencil": lax.div(device, self.cores), "tgroup": lax.rem(device, self.cores)}

    def greet(self):
        @pl.loop(1, self.count)
        def _(step):
            pl.semaphore_signal(
                self.barrier,
                inc=1,
                device_id=self.name(self.at(step)),
                device_id_type=pl.DeviceIdType.MESH,
            )

    def met(self):
        pl.semaphore_wait(self.barrier, self.count - 1)

    def copy(self, step, source, target, sent, got):
        peer = self.at(step)
        return pltpu.make_async_remote_copy(
            src_ref=source.at[peer],
            dst_ref=target.at[self.me],
            send_sem=sent.at[step],
            recv_sem=got.at[step],
            device_id=self.name(peer),
            device_id_type=pl.DeviceIdType.MESH,
        )

    def settle(self, source, target, sent, got):
        @pl.loop(1, self.count)
        def _(step):
            self.copy(step, source, target, sent, got).wait()


def depth_up(
    coeff_ref,
    pw_ref,
    table_ref,
    out_ref,
    ready,
    coeff,
    inverse,
    column,
    sent,
    got,
):
    peers = Peers()
    peers.greet()
    bands = coeff_ref.shape[1]
    _, _, rows, width = coeff.shape
    devices, part_rows, _ = out_ref.shape
    zpw, own = pw_ref.shape
    length = inverse.shape[1]
    for part in range(2):
        for band in range(bands):
            for start in range(0, rows, 3 * GROUP // 2):
                some = range(start, min(start + 3 * GROUP // 2, rows))
                values = [
                    coeff_ref[part, band : band + 1, row * width : (row + 1) * width]
                    for row in some
                ]
                for row, value in zip(some, values):
                    coeff[part, band, row : row + 1] = value
    z = lax.broadcasted_iota(jnp.int32, (length, LANES), 0)
    for tile in range(own // LANES + (own % LANES > 0)):
        lanes = slice(tile * LANES, min((tile + 1) * LANES, own))
        source = jnp.full((length, LANES), -1, jnp.int32)
        for k in range(zpw):
            row = pw_ref[k : k + 1, lanes]
            if row.shape[1] < LANES:
                row = jnp.concatenate(
                    [row, jnp.full((1, LANES - row.shape[1]), -1, jnp.int32)], axis=1
                )
            source = jnp.where(row == z, k, source)
        inverse[tile * LANES : (tile + 1) * LANES] = source.T
    for parity in range(2):
        source = inverse[pl.ds(parity, rows, stride=2), :]
        found = source >= 0
        source = jnp.maximum(source, 0) + parity * zpw
        for band in range(bands):
            places = pl.ds(band * own + parity, rows, stride=2)
            for part in range(2):
                taken = jnp.take_along_axis(
                    coeff[part, band], source, axis=1, mode="promise_in_bounds"
                )
                column[part, places, :] = jnp.where(found, taken, 0.0)
    value = jnp.concatenate([column[0], column[1]], axis=1)
    field = dot3((table_ref[0], table_ref[1]), split(value), ((1,), (1,)))
    for device in range(devices):
        ready[device] = field[device * part_rows : (device + 1) * part_rows]
    peers.met()

    @pl.loop(1, devices)
    def _(turn):
        peers.copy(peers.step(turn), ready, out_ref, sent, got).start()

    out_ref[peers.me] = ready[peers.me]
    peers.settle(ready, out_ref, sent, got)


def turn(value):
    half = value.shape[0] // 2
    return jnp.concatenate([-value[half:], value[:half]], axis=0)


def row_product(pair, table):
    length = table.shape[1] // 2
    mul = partial(jnp.dot, preferred_element_type=F32)
    both = mul(pair[0], table[...])
    return both[:, :length] + (both[:, length:] + mul(pair[1], table[:, :length]))


def plane_kernel(
    bands,
    cols_ref,
    field_ref,
    weight_ref,
    table_ref,
    out_ref,
    flat,
    sticks,
    grid,
    other,
):
    devices, part_rows, block = field_ref.shape
    planes = part_rows // 2
    own = block // bands
    length = weight_ref.shape[1]
    bz = bands * planes
    slots = LANES // (2 * bz)
    inner = length // slots
    group_rows = inner * length
    batch = math.gcd(inner, 8)
    total = devices * own

    grid[...] = jnp.zeros_like(grid)
    for part in range(2):
        for band in range(bands):
            start = (part * bands + band) * planes
            values = [
                field_ref[
                    device, part * planes : (part + 1) * planes, band * own : (band + 1) * own
                ]
                for device in range(devices)
            ]
            for device, value in enumerate(values):
                flat[start : start + planes, device * own : (device + 1) * own] = value
    for start in range(0, total // LANES, 6):
        some = range(start, min(start + 6, total // LANES))
        values = [flat[:, tile * LANES : (tile + 1) * LANES] for tile in some]
        for tile, value in zip(some, values):
            value = jnp.concatenate([value[:bz]] * slots + [value[bz:]] * slots, axis=0)
            sticks[tile * LANES : (tile + 1) * LANES] = value.T

    lane = lax.broadcasted_iota(jnp.int32, (1, LANES), 1)
    first_of_lane = (lane // bz % slots) * group_rows
    group = math.gcd(total, 3 * GROUP // 2)

    @pl.loop(0, total // group)
    def _(step):
        base = pl.multiple_of(step * group, group)
        cols = [cols_ref[base + i] for i in range(group)]
        values = [sticks[pl.ds(base + i, 1), :] for i in range(group)]
        for col, value in zip(cols, values):
            spread = jnp.full((1, LANES), col, jnp.int32)
            mask = (spread & -group_rows) == first_of_lane
            pltpu.store(grid.at[pl.ds(col & (group_rows - 1), 1), :], value, mask=mask)

    @pl.loop(0, inner // batch)
    def _(step):
        whole = pl.ds(pl.multiple_of(step * batch * length, batch * length), batch * length)
        his, los = [], []
        for i in range(batch):
            start = pl.multiple_of((step * batch + i) * length, length)
            hi, lo = split(grid[pl.ds(start, length), :].T)
            his.append(jnp.concatenate([hi, turn(hi)], axis=1))
            los.append(jnp.concatenate([lo, turn(lo)], axis=1))
        pair = (jnp.concatenate(his, axis=0), jnp.concatenate(los, axis=0))
        other[whole, :] = row_product(pair, table_ref[2])

    def picks(z):
        return [pl.ds(band * planes + z, 2 * length, stride=bz) for band in range(bands)]

    def planes_of(z):
        return split(jnp.concatenate([other[pick, :] for pick in picks(z)], axis=1))

    following = planes_of(0)
    for z in range(planes):
        value = dot3((table_ref[4], table_ref[5]), following)
        if z + 1 < planes:
            following = planes_of(z + 1)
        weight = weight_ref[pl.ds(z, length, stride=planes), :]
        weight = jnp.concatenate([weight] * 2, axis=0)
        weight = jnp.concatenate([weight] * bands, axis=1)
        value = dot3((table_ref[6], table_ref[7]), split(value * weight))
        for band, pick in enumerate(picks(z)):
            grid[pick, :] = value[:, band * length : (band + 1) * length]

    @pl.loop(0, inner // batch)
    def _(step):
        his, los = [], []
        starts = [pl.multiple_of((step * batch + i) * length, length) for i in range(batch)]
        for start in starts:
            hi, lo = split(grid[pl.ds(start, length), :])
            his.append(jnp.concatenate([hi, turn(hi)], axis=1))
            los.append(jnp.concatenate([lo, turn(lo)], axis=1))
        pair = (jnp.concatenate(his, axis=0), jnp.concatenate(los, axis=0))
        value = row_product(pair, table_ref[3])
        for i, start in enumerate(starts):
            out_ref[pl.ds(start, length), :] = value[i * length : (i + 1) * length].T


def depth_down(
    cols_ref,
    slot_ref,
    grid_ref,
    pw_ref,
    table_ref,
    out_ref,
    ready,
    field,
    sticks,
    flat,
    column,
    sent,
    got,
):
    peers = Peers()
    peers.greet()
    _, bands, rows, width = out_ref.shape
    devices, part_rows, _ = ready.shape
    planes = part_rows // 2
    own = 2 * rows
    length = devices * planes
    bz = bands * planes
    slots = LANES // (2 * bz)
    half = slots * bz
    group_rows = grid_ref.shape[0]
    shift = group_rows.bit_length() - 1
    group = math.gcd(own, GROUP // 2)

    def gather(device):
        def fetch(chunk):
            first = device * own + chunk * group
            cols = [cols_ref[first + i] for i in range(group)]
            return [grid_ref[pl.ds(col & (group_rows - 1), 1), :] for col in cols]

        def put(chunk, values):
            start = pl.multiple_of(chunk * group, group)
            for i, value in enumerate(values):
                sticks[pl.ds(start + i, 1), :] = value

        def each(chunk, held):
            following = fetch(chunk)
            put(chunk - 1, held)
            return following

        chunks = own // group
        put(chunks - 1, lax.fori_loop(1, chunks, each, fetch(0)))

        slot_of = lax.shift_right_logical(slot_ref[device], shift)

        tiles = []
        for tile in range(sticks.shape[0] // LANES):
            value = sticks[tile * LANES : (tile + 1) * LANES].T
            here = slot_of[:, tile * LANES : (tile + 1) * LANES]
            sums = []
            for part in range(2):
                total = value[part * half : part * half + bz]
                for slot in range(1, slots):
                    start = part * half + slot * bz
                    total = jnp.where(here == slot, value[start : start + bz], total)
                sums.append(total)
            tiles.append(jnp.concatenate(sums, axis=0))
        value = jnp.concatenate(tiles, axis=1)[:, :own]
        for part in range(2):
            for band in range(bands):
                start = (part * bands + band) * planes
                ready[
                    device, part * planes : (part + 1) * planes, band * own : (band + 1) * own
                ] = value[start : start + planes]

    sticks[...] = jnp.zeros_like(sticks)
    gather(peers.at(peers.step(1)))
    peers.met()
    peers.copy(peers.step(1), ready, field, sent, got).start()

    @pl.loop(2, devices)
    def _(turn):
        step = peers.step(turn)
        gather(peers.at(step))
        peers.copy(step, ready, field, sent, got).start()

    gather(peers.me)
    field[peers.me] = ready[peers.me]
    pw = pw_ref[...]
    first = lax.broadcasted_iota(jnp.int32, (rows, LANES), 1) < width // 2
    peers.settle(ready, field, sent, got)
    for device in range(devices):
        flat[device * part_rows : (device + 1) * part_rows] = field[device]
    value = dot3(split(flat[...]), (table_ref[0], table_ref[1]), ((0,), (0,)))
    column[0] = value[:, :length]
    column[1] = value[:, length:]
    for band in range(bands):
        for part in range(2):
            taken = []
            for parity in range(2):
                piece = column[part, pl.ds(band * own + parity, rows, stride=2), :]
                taken.append(
                    jnp.take_along_axis(piece, pw, axis=1, mode="promise_in_bounds")
                )
            out_ref[part, band] = jnp.where(first, taken[0], taken[1])


VM = pl.BlockSpec(memory_space=pltpu.VMEM)
SM = pl.BlockSpec(memory_space=pltpu.SMEM)
params = partial(pltpu.CompilerParams, vmem_limit_bytes=40 * 1024 * 1024)


def local(dpsi, stick_cols, pw_z, v_local, dv):
    devices = lax.axis_size("pencil") * lax.axis_size("tgroup")
    cores = lax.axis_size("tgroup")
    core = lax.axis_index("tgroup")
    length = math.isqrt(v_local.shape[1])
    planes = v_local.shape[0] // cores
    own = pw_z.shape[0] // cores
    zpw = pw_z.shape[1]
    bands = dpsi.shape[1]
    pairs = own // 2
    bz = bands * planes
    slots = LANES // (2 * bz)

    rows = lax.dynamic_slice_in_dim(pw_z, core * own, own, 0).reshape(pairs, 2 * zpw)
    coeff = (2, bands, pairs, 2 * zpw)
    by_wave = lax.dynamic_slice_in_dim(pw_z.T, core * own, own, 1)

    column = column_table(length, slots)
    tables = list(halves(depth_table(length, devices)))
    tables += [np.concatenate(halves(table), axis=1) for table in row_tables(length)]
    tables += halves(column) + halves(np.ascontiguousarray(column.T))
    tables = jnp.asarray(np.stack(tables))
    potential = lax.dynamic_slice_in_dim(v_local, core * planes, planes, 0)
    potential = potential + lax.dynamic_slice_in_dim(dv, core * planes, planes, 0)
    potential = potential.reshape(planes, length, length).transpose(1, 0, 2)
    by_wave, potential = lax.optimization_barrier((by_wave, potential))
    potential = potential.reshape(length * planes, length)

    slot_cols = jnp.pad(stick_cols.reshape(devices, 1, own), ((0, 0), (0, 0), (0, -own % LANES)))
    block = (devices, 2 * planes, bands * own)
    in_slots = length // slots * length
    padded = -(-own // LANES) * LANES
    cost = pl.CostEstimate(
        flops=0, bytes_accessed=100 * math.prod(block) * 4, transcendentals=0
    )
    field = pl.pallas_call(
        depth_up,
        out_shape=jax.ShapeDtypeStruct(block, F32),
        in_specs=[VM] * 3,
        out_specs=VM,
        scratch_shapes=[
            pltpu.VMEM(block, F32),
            pltpu.VMEM(coeff, F32),
            pltpu.VMEM((padded, length), jnp.int32),
            pltpu.VMEM((2, bands * own, length), F32),
            pltpu.SemaphoreType.DMA((devices,)),
            pltpu.SemaphoreType.DMA((devices,)),
        ],
        cost_estimate=cost,
        compiler_params=params(collective_id=0, has_side_effects=True),
    )(dpsi, by_wave, tables)
    grid = pl.pallas_call(
        partial(plane_kernel, bands),
        out_shape=jax.ShapeDtypeStruct((in_slots, LANES), F32),
        in_specs=[SM] + [VM] * 3,
        out_specs=VM,
        scratch_shapes=[
            pltpu.VMEM((2 * bz, devices * own), F32),
            pltpu.VMEM((devices * own, LANES), F32),
            pltpu.VMEM((in_slots, LANES), F32),
            pltpu.VMEM((in_slots, LANES), F32),
        ],
        cost_estimate=cost,
        compiler_params=params(),
    )(stick_cols, field, potential, tables)
    output = pl.pallas_call(
        depth_down,
        out_shape=jax.ShapeDtypeStruct(coeff, F32),
        in_specs=[SM] + [VM] * 4,
        out_specs=VM,
        scratch_shapes=[
            pltpu.VMEM(block, F32),
            pltpu.VMEM(block, F32),
            pltpu.VMEM((padded, LANES), F32),
            pltpu.VMEM((2 * length, bands * own), F32),
            pltpu.VMEM((2, bands * own, length), F32),
            pltpu.SemaphoreType.DMA((devices,)),
            pltpu.SemaphoreType.DMA((devices,)),
        ],
        cost_estimate=cost,
        compiler_params=params(collective_id=1, has_side_effects=True),
    )(stick_cols, slot_cols, grid, rows, tables)
    return output.reshape(dpsi.shape)


def solution(mesh):
    in_specs = (
        P(None, "pool", ("pencil", "tgroup")),
        P(),
        P("pencil", None),
        P("pencil", None),
        P("pencil", None),
    )
    out_specs = P(None, "pool", ("pencil", "tgroup"))
    return jax.shard_map(local, mesh=mesh, in_specs=in_specs, out_specs=out_specs, check_vma=False)
```

```python
from functools import partial
import math

import jax
import jax.numpy as jnp
import ml_dtypes
import numpy as np
from jax import lax
from jax.experimental import pallas as pl
from jax.experimental.pallas import tpu as pltpu
from jax.sharding import PartitionSpec as P

F32 = jnp.float32
BF16 = jnp.bfloat16
LANES = 128
GROUP = 32


def halves(table):
    hi = table.astype(ml_dtypes.bfloat16)
    lo = (table - hi.astype(np.float64)).astype(ml_dtypes.bfloat16)
    return hi, lo


def split(value):
    hi = value.astype(BF16)
    lo = (value - hi.astype(F32)).astype(BF16)
    return hi, lo


def dot3(left, right, dims=((1,), (0,))):
    mul = lambda a, b: lax.dot_general(a, b, (dims, ((), ())), preferred_element_type=F32)
    return mul(left[0], right[0]) + (mul(left[0], right[1]) + mul(left[1], right[0]))


def waves(length):
    k = np.arange(length)
    angle = (k[:, None] * k[None, :] % length) * (2.0 * math.pi / length)
    return np.cos(angle) / math.sqrt(length), np.sin(angle) / math.sqrt(length)


def depth_table(length, devices):
    cos, sin = waves(length)
    planes = length // devices
    whole = np.stack([np.stack([cos, -sin], 1), np.stack([sin, cos], 1)])
    whole = whole.reshape(2, devices, planes, 2 * length)
    return whole.transpose(1, 0, 2, 3).reshape(2 * length, 2 * length)


def row_tables(length):
    cos, sin = waves(length)
    return np.concatenate([cos, sin]), np.concatenate([cos, -sin])


def column_table(length, slots):
    cos, sin = waves(length)
    whole = np.stack([np.stack([cos, -sin], 1), np.stack([sin, cos], 1)])
    whole = whole.reshape(2, length, 2, slots, length // slots)
    return whole.transpose(0, 1, 4, 2, 3).reshape(2 * length, 2 * length)


class Peers:
    def __init__(self):
        self.cores = lax.axis_size("tgroup")
        self.count = lax.axis_size("pencil") * self.cores
        self.me = lax.axis_index("pencil") * self.cores + lax.axis_index("tgroup")
        self.barrier = pltpu.get_barrier_semaphore()

    def at(self, step):
        return lax.rem(self.me + step, self.count)

    def step(self, turn):
        away = lax.div(turn, 2)
        return self.count // 2 + jnp.where(lax.rem(turn, 2) == 0, away, -away)

    def name(self, device):
        return {"pencil": lax.div(device, self.cores), "tgroup": lax.rem(device, self.cores)}

    def greet(self):
        @pl.loop(1, self.count)
        def _(step):
            pl.semaphore_signal(
                self.barrier,
                inc=1,
                device_id=self.name(self.at(step)),
                device_id_type=pl.DeviceIdType.MESH,
            )

    def met(self):
        pl.semaphore_wait(self.barrier, self.count - 1)

    def copy(self, step, source, target, sent, got):
        peer = self.at(step)
        return pltpu.make_async_remote_copy(
            src_ref=source.at[peer],
            dst_ref=target.at[self.me],
            send_sem=sent.at[step],
            recv_sem=got.at[step],
            device_id=self.name(peer),
            device_id_type=pl.DeviceIdType.MESH,
        )

    def settle(self, source, target, sent, got):
        @pl.loop(1, self.count)
        def _(step):
            self.copy(step, source, target, sent, got).wait()


def depth_up(
    coeff_ref,
    pw_ref,
    table_ref,
    out_ref,
    ready,
    coeff,
    inverse,
    column,
    sent,
    got,
):
    peers = Peers()
    peers.greet()
    bands = coeff_ref.shape[1]
    _, _, rows, width = coeff.shape
    devices, part_rows, _ = out_ref.shape
    zpw, own = pw_ref.shape
    length = inverse.shape[1]
    for part in range(2):
        for band in range(bands):
            for start in range(0, rows, 3 * GROUP // 2):
                some = range(start, min(start + 3 * GROUP // 2, rows))
                values = [
                    coeff_ref[part, band : band + 1, row * width : (row + 1) * width]
                    for row in some
                ]
                for row, value in zip(some, values):
                    coeff[part, band, row : row + 1] = value
    z = lax.broadcasted_iota(jnp.int32, (length, LANES), 0)
    for tile in range(own // LANES + (own % LANES > 0)):
        lanes = slice(tile * LANES, min((tile + 1) * LANES, own))
        source = jnp.full((length, LANES), -1, jnp.int32)
        for k in range(zpw):
            row = pw_ref[k : k + 1, lanes]
            if row.shape[1] < LANES:
                row = jnp.concatenate(
                    [row, jnp.full((1, LANES - row.shape[1]), -1, jnp.int32)], axis=1
                )
            source = jnp.where(row == z, k, source)
        inverse[tile * LANES : (tile + 1) * LANES] = source.T
    for parity in range(2):
        source = inverse[pl.ds(parity, rows, stride=2), :]
        found = source >= 0
        source = jnp.maximum(source, 0) + parity * zpw
        for band in range(bands):
            places = pl.ds(band * own + parity, rows, stride=2)
            for part in range(2):
                taken = jnp.take_along_axis(
                    coeff[part, band], source, axis=1, mode="promise_in_bounds"
                )
                column[part, places, :] = jnp.where(found, taken, 0.0)
    value = jnp.concatenate([column[0], column[1]], axis=1)
    field = dot3((table_ref[0], table_ref[1]), split(value), ((1,), (1,)))
    for device in range(devices):
        ready[device] = field[device * part_rows : (device + 1) * part_rows]
    peers.met()

    @pl.loop(1, devices)
    def _(turn):
        peers.copy(peers.step(turn), ready, out_ref, sent, got).start()

    out_ref[peers.me] = ready[peers.me]
    peers.settle(ready, out_ref, sent, got)


def turn(value):
    half = value.shape[0] // 2
    return jnp.concatenate([-value[half:], value[:half]], axis=0)


def row_product(pair, table):
    length = table.shape[1] // 2
    mul = partial(jnp.dot, preferred_element_type=F32)
    both = mul(pair[0], table[...])
    return both[:, :length] + (both[:, length:] + mul(pair[1], table[:, :length]))


def plane_kernel(
    bands,
    cols_ref,
    field_ref,
    weight_ref,
    table_ref,
    out_ref,
    flat,
    sticks,
    grid,
    other,
):
    devices, part_rows, block = field_ref.shape
    planes = part_rows // 2
    own = block // bands
    length = weight_ref.shape[1]
    bz = bands * planes
    slots = LANES // (2 * bz)
    inner = length // slots
    group_rows = inner * length
    batch = math.gcd(inner, 8)
    total = devices * own

    grid[...] = jnp.zeros_like(grid)
    for part in range(2):
        for band in range(bands):
            start = (part * bands + band) * planes
            values = [
                field_ref[
                    device, part * planes : (part + 1) * planes, band * own : (band + 1) * own
                ]
                for device in range(devices)
            ]
            for device, value in enumerate(values):
                flat[start : start + planes, device * own : (device + 1) * own] = value
    for start in range(0, total // LANES, 6):
        some = range(start, min(start + 6, total // LANES))
        values = [flat[:, tile * LANES : (tile + 1) * LANES] for tile in some]
        for tile, value in zip(some, values):
            value = jnp.concatenate([value[:bz]] * slots + [value[bz:]] * slots, axis=0)
            sticks[tile * LANES : (tile + 1) * LANES] = value.T

    lane = lax.broadcasted_iota(jnp.int32, (1, LANES), 1)
    first_of_lane = (lane // bz % slots) * group_rows
    group = math.gcd(total, 3 * GROUP // 2)

    @pl.loop(0, total // group)
    def _(step):
        base = pl.multiple_of(step * group, group)
        cols = [cols_ref[base + i] for i in range(group)]
        values = [sticks[pl.ds(base + i, 1), :] for i in range(group)]
        for col, value in zip(cols, values):
            spread = jnp.full((1, LANES), col, jnp.int32)
            mask = (spread & -group_rows) == first_of_lane
            pltpu.store(grid.at[pl.ds(col & (group_rows - 1), 1), :], value, mask=mask)

    @pl.loop(0, inner // batch)
    def _(step):
        whole = pl.ds(pl.multiple_of(step * batch * length, batch * length), batch * length)
        his, los = [], []
        for i in range(batch):
            start = pl.multiple_of((step * batch + i) * length, length)
            hi, lo = split(grid[pl.ds(start, length), :].T)
            his.append(jnp.concatenate([hi, turn(hi)], axis=1))
            los.append(jnp.concatenate([lo, turn(lo)], axis=1))
        pair = (jnp.concatenate(his, axis=0), jnp.concatenate(los, axis=0))
        other[whole, :] = row_product(pair, table_ref[2])

    def picks(z):
        return [pl.ds(band * planes + z, 2 * length, stride=bz) for band in range(bands)]

    def planes_of(z):
        return split(jnp.concatenate([other[pick, :] for pick in picks(z)], axis=1))

    following = planes_of(0)
    for z in range(planes):
        value = dot3((table_ref[4], table_ref[5]), following)
        if z + 1 < planes:
            following = planes_of(z + 1)
        weight = weight_ref[pl.ds(z, length, stride=planes), :]
        weight = jnp.concatenate([weight] * 2, axis=0)
        weight = jnp.concatenate([weight] * bands, axis=1)
        value = dot3((table_ref[6], table_ref[7]), split(value * weight))
        for band, pick in enumerate(picks(z)):
            grid[pick, :] = value[:, band * length : (band + 1) * length]

    @pl.loop(0, inner // batch)
    def _(step):
        his, los = [], []
        starts = [pl.multiple_of((step * batch + i) * length, length) for i in range(batch)]
        for start in starts:
            hi, lo = split(grid[pl.ds(start, length), :])
            his.append(jnp.concatenate([hi, turn(hi)], axis=1))
            los.append(jnp.concatenate([lo, turn(lo)], axis=1))
        pair = (jnp.concatenate(his, axis=0), jnp.concatenate(los, axis=0))
        value = row_product(pair, table_ref[3])
        for i, start in enumerate(starts):
            out_ref[pl.ds(start, length), :] = value[i * length : (i + 1) * length].T


def depth_down(
    cols_ref,
    slot_ref,
    grid_ref,
    pw_ref,
    table_ref,
    out_ref,
    ready,
    field,
    sticks,
    flat,
    column,
    sent,
    got,
):
    peers = Peers()
    peers.greet()
    _, bands, rows, width = out_ref.shape
    devices, part_rows, _ = ready.shape
    planes = part_rows // 2
    own = 2 * rows
    length = devices * planes
    bz = bands * planes
    slots = LANES // (2 * bz)
    half = slots * bz
    group_rows = grid_ref.shape[0]
    shift = group_rows.bit_length() - 1
    group = math.gcd(own, GROUP // 2)

    def gather(device):
        def fetch(chunk):
            first = device * own + chunk * group
            cols = [cols_ref[first + i] for i in range(group)]
            return [grid_ref[pl.ds(col & (group_rows - 1), 1), :] for col in cols]

        def put(chunk, values):
            start = pl.multiple_of(chunk * group, group)
            for i, value in enumerate(values):
                sticks[pl.ds(start + i, 1), :] = value

        def each(chunk, held):
            following = fetch(chunk)
            put(chunk - 1, held)
            return following

        chunks = own // group
        put(chunks - 1, lax.fori_loop(1, chunks, each, fetch(0)))

        slot_of = lax.shift_right_logical(slot_ref[device], shift)

        tiles = []
        for tile in range(sticks.shape[0] // LANES):
            value = sticks[tile * LANES : (tile + 1) * LANES].T
            here = slot_of[:, tile * LANES : (tile + 1) * LANES]
            sums = []
            for part in range(2):
                total = value[part * half : part * half + bz]
                for slot in range(1, slots):
                    start = part * half + slot * bz
                    total = jnp.where(here == slot, value[start : start + bz], total)
                sums.append(total)
            tiles.append(jnp.concatenate(sums, axis=0))
        value = jnp.concatenate(tiles, axis=1)[:, :own]
        for part in range(2):
            for band in range(bands):
                start = (part * bands + band) * planes
                ready[
                    device, part * planes : (part + 1) * planes, band * own : (band + 1) * own
                ] = value[start : start + planes]

    sticks[...] = jnp.zeros_like(sticks)
    gather(peers.at(peers.step(1)))
    peers.met()
    peers.copy(peers.step(1), ready, field, sent, got).start()

    @pl.loop(2, devices)
    def _(turn):
        step = peers.step(turn)
        gather(peers.at(step))
        peers.copy(step, ready, field, sent, got).start()

    gather(peers.me)
    field[peers.me] = ready[peers.me]
    pw = pw_ref[...]
    first = lax.broadcasted_iota(jnp.int32, (rows, LANES), 1) < width // 2
    peers.settle(ready, field, sent, got)
    for device in range(devices):
        flat[device * part_rows : (device + 1) * part_rows] = field[device]
    value = dot3(split(flat[...]), (table_ref[0], table_ref[1]), ((0,), (0,)))
    column[0] = value[:, :length]
    column[1] = value[:, length:]
    for band in range(bands):
        for part in range(2):
            taken = []
            for parity in range(2):
                piece = column[part, pl.ds(band * own + parity, rows, stride=2), :]
                taken.append(
                    jnp.take_along_axis(piece, pw, axis=1, mode="promise_in_bounds")
                )
            out_ref[part, band] = jnp.where(first, taken[0], taken[1])


VM = pl.BlockSpec(memory_space=pltpu.VMEM)
SM = pl.BlockSpec(memory_space=pltpu.SMEM)
params = partial(pltpu.CompilerParams, vmem_limit_bytes=40 * 1024 * 1024)


def local(dpsi, stick_cols, pw_z, v_local, dv):
    devices = lax.axis_size("pencil") * lax.axis_size("tgroup")
    cores = lax.axis_size("tgroup")
    core = lax.axis_index("tgroup")
    length = math.isqrt(v_local.shape[1])
    planes = v_local.shape[0] // cores
    own = pw_z.shape[0] // cores
    zpw = pw_z.shape[1]
    bands = dpsi.shape[1]
    pairs = own // 2
    bz = bands * planes
    slots = LANES // (2 * bz)

    potential = lax.dynamic_slice_in_dim(v_local, core * planes, planes, 0)
    potential = potential + lax.dynamic_slice_in_dim(dv, core * planes, planes, 0)
    potential = potential.reshape(planes, length, length).transpose(1, 0, 2)
    pw_z, potential = lax.optimization_barrier((pw_z, potential))
    rows = lax.dynamic_slice_in_dim(pw_z, core * own, own, 0).reshape(pairs, 2 * zpw)
    coeff = (2, bands, pairs, 2 * zpw)
    by_wave = lax.dynamic_slice_in_dim(pw_z.T, core * own, own, 1)

    column = column_table(length, slots)
    tables = list(halves(depth_table(length, devices)))
    tables += [np.concatenate(halves(table), axis=1) for table in row_tables(length)]
    tables += halves(column) + halves(np.ascontiguousarray(column.T))
    tables = jnp.asarray(np.stack(tables))
    potential = potential.reshape(length * planes, length)

    slot_cols = jnp.pad(stick_cols.reshape(devices, 1, own), ((0, 0), (0, 0), (0, -own % LANES)))
    block = (devices, 2 * planes, bands * own)
    in_slots = length // slots * length
    padded = -(-own // LANES) * LANES
    cost = pl.CostEstimate(
        flops=0, bytes_accessed=100 * math.prod(block) * 4, transcendentals=0
    )
    field = pl.pallas_call(
        depth_up,
        out_shape=jax.ShapeDtypeStruct(block, F32),
        in_specs=[VM] * 3,
        out_specs=VM,
        scratch_shapes=[
            pltpu.VMEM(block, F32),
            pltpu.VMEM(coeff, F32),
            pltpu.VMEM((padded, length), jnp.int32),
            pltpu.VMEM((2, bands * own, length), F32),
            pltpu.SemaphoreType.DMA((devices,)),
            pltpu.SemaphoreType.DMA((devices,)),
        ],
        cost_estimate=cost,
        compiler_params=params(collective_id=0, has_side_effects=True),
    )(dpsi, by_wave, tables)
    grid = pl.pallas_call(
        partial(plane_kernel, bands),
        out_shape=jax.ShapeDtypeStruct((in_slots, LANES), F32),
        in_specs=[SM] + [VM] * 3,
        out_specs=VM,
        scratch_shapes=[
            pltpu.VMEM((2 * bz, devices * own), F32),
            pltpu.VMEM((devices * own, LANES), F32),
            pltpu.VMEM((in_slots, LANES), F32),
            pltpu.VMEM((in_slots, LANES), F32),
        ],
        cost_estimate=cost,
        compiler_params=params(),
    )(stick_cols, field, potential, tables)
    output = pl.pallas_call(
        depth_down,
        out_shape=jax.ShapeDtypeStruct(coeff, F32),
        in_specs=[SM] + [VM] * 4,
        out_specs=VM,
        scratch_shapes=[
            pltpu.VMEM(block, F32),
            pltpu.VMEM(block, F32),
            pltpu.VMEM((padded, LANES), F32),
            pltpu.VMEM((2 * length, bands * own), F32),
            pltpu.VMEM((2, bands * own, length), F32),
            pltpu.SemaphoreType.DMA((devices,)),
            pltpu.SemaphoreType.DMA((devices,)),
        ],
        cost_estimate=cost,
        compiler_params=params(collective_id=1, has_side_effects=True),
    )(stick_cols, slot_cols, grid, rows, tables)
    return output.reshape(dpsi.shape)


def solution(mesh):
    in_specs = (
        P(None, "pool", ("pencil", "tgroup")),
        P(),
        P("pencil", None),
        P("pencil", None),
        P("pencil", None),
    )
    out_specs = P(None, "pool", ("pencil", "tgroup"))
    return jax.shard_map(local, mesh=mesh, in_specs=in_specs, out_specs=out_specs, check_vma=False)
```
